256 devices in a mesh: step: 64 (over z, y, core), quad: 4 (over x).
Axes of the slice: x: 4, y: 4, z: 8, core: 2. Of those that a mesh axis runs over, the one named last changes fastest.
Arguments:
- states: float32 [64, 3, 256, 256], P('step', None, 'quad'), may hold values from -6 to 6
- noise_field: float32 [64, 3, 256, 256], P('step', None, 'quad'), may hold values from -6 to 6
- window_start: int32 [1], replicated, may hold values from 0 to 935
- patch_weight: bfloat16 [192, 512], replicated, may hold values from -0.4375 to 0.4375
- time_weight: bfloat16 [128, 1024], replicated, may hold values from -0.5 to 0.5
- conv_first: bfloat16 [3, 3, 512, 512], replicated, may hold values from -0.09375 to 0.09375
- conv_second: bfloat16 [3, 3, 512, 512], replicated, may hold values from -0.09375 to 0.09375
- attn_weight: bfloat16 [512, 1536], replicated, may hold values from -0.5 to 0.5
- proj_weight: bfloat16 [512, 512], replicated, may hold values from -0.25 to 0.25
- out_weight: bfloat16 [512, 192], replicated, may hold values from -0.5 to 0.5
Outputs:
- new_states: float32 [64, 3, 256, 256], P('step', None, 'quad')
The draws below stay inside these ranges and needn't reach their ends.
All inputs are finite; a program needn't handle non-finite values.
Results may differ from the reference program's by a relative error of at most 0.0025.
Values may be sent and summed in bfloat16 or wider, within the bound.
A program may use at most 128 MiB of HBM per device.

```python
import math
import jax
import jax.numpy as jnp
from jax import lax

IMG = 256
CH = 512
HEAD_DIM = 64
GROUPS = 32
PATCH = 8
TEMB = 128
HEADS = 8
STEPS = 64


def level_of(key, extent, shards, least, high):
    def one(position, blocks):
        heights = jax.random.uniform(jax.random.fold_in(jax.random.fold_in(key, 6), position), (blocks,), jnp.float32, least / len(shards), high / len(shards))
        return jnp.repeat(jnp.exp(heights), extent[position] // blocks).reshape((-1,) + (1,) * (len(extent) - position - 1))

    factor_of = one(*shards[0])
    for cut in shards[1:]:
        factor_of = factor_of * one(*cut)
    return factor_of


def bell_draw(rng, dims, spread, bound, pieces=(), kind=jnp.bfloat16):
    drawn = jax.random.normal(rng, dims, jnp.float32) * spread
    if len(pieces) > 0:
        drawn = level_of(rng, dims, pieces, -0.22, 0.18) * drawn
    return jnp.clip(drawn, min=-bound, max=bound).astype(kind)


def setup_inputs(seed: int = 0) -> dict:
    seeds = jax.random.split(jax.random.key(seed), 11)
    return {
        "states": bell_draw(seeds[0], (STEPS, 3, IMG, IMG), 1.0, 6.0, ((0, 64), (2, 4)), jnp.float32),
        "noise_field": bell_draw(seeds[1], (STEPS, 3, IMG, IMG), 1.0, 6.0, ((0, 64), (2, 4)), jnp.float32),
        "window_start": jax.random.randint(seeds[2], (1,), 0, 1000 - STEPS).astype(jnp.int32),
        "patch_weight": bell_draw(seeds[3], (3 * PATCH * PATCH, CH), (3 * PATCH * PATCH) ** -0.5, 0.4375),
        "time_weight": bell_draw(seeds[4], (TEMB, 2 * CH), TEMB ** -0.5, 0.5),
        "conv_first": bell_draw(seeds[5], (3, 3, CH, CH), (9 * CH) ** -0.5, 0.09375),
        "conv_second": bell_draw(seeds[6], (3, 3, CH, CH), (9 * CH) ** -0.5, 0.09375),
        "attn_weight": bell_draw(seeds[7], (CH, 3 * CH), (CH // 4) ** -0.5, 0.5),
        "proj_weight": bell_draw(seeds[8], (CH, CH), CH ** -0.5, 0.25),
        "out_weight": bell_draw(seeds[9], (CH, 3 * PATCH * PATCH), (CH // 4) ** -0.5, 0.5),
    }


epsilon_norm = 1e-05

def plan(step_time):
    positions = jnp.arange(1000, dtype=jnp.float32)
    beta_table = 0.0001 + (0.02 - 0.0001) * positions / 999.0
    log_keep = jnp.cumsum(jnp.log(1.0 - beta_table))
    chosen = jnp.arange(1000, dtype=jnp.int32) == step_time
    beta_now = jnp.sum(jnp.where(chosen, beta_table, jnp.zeros_like(beta_table)))
    log_now = jnp.sum(jnp.where(chosen, log_keep, jnp.zeros_like(log_keep)))
    return (beta_now, jnp.exp(log_now))

def time_embedding(step_time, width):
    half_width = width // 2
    frequency = jnp.exp(-math.log(10000.0) * jnp.arange(half_width, dtype=jnp.float32) / half_width)
    angles = step_time.astype(jnp.float32) * frequency
    return jnp.concatenate([jnp.cos(angles), jnp.sin(angles)]).astype(jnp.bfloat16)

def group_norm(hidden):
    rows, channels = hidden.shape
    view = hidden.reshape(rows, GROUPS, channels // GROUPS)
    average = lax.optimization_barrier(jnp.mean(view, axis=(0, 2)))
    square_avg = lax.optimization_barrier(jnp.mean(view * view, axis=(0, 2)))
    variance = square_avg - average * average
    normed = (view - average[None, :, None]) * lax.rsqrt(variance + epsilon_norm)[None, :, None]
    return normed.reshape(rows, channels)

def convolve(acts, weight):
    grid_rows, grid_cols, channels = acts.shape
    padded = jnp.pad(acts, ((1, 1), (1, 1), (0, 0)))
    total = jnp.zeros((grid_rows * grid_cols, weight.shape[3]), jnp.float32)
    for row_off in range(3):
        for col_off in range(3):
            window = padded[row_off:row_off + grid_rows, col_off:col_off + grid_cols].reshape(-1, channels)
            total = total + jnp.dot(window, weight[row_off, col_off], preferred_element_type=jnp.float32)
    return total

def denoiser(field, step_time, patch_weight, time_weight, conv_first, conv_second, attn_weight, proj_weight, out_weight):
    grid = field.shape[1] // PATCH
    patches = field.reshape(3, grid, PATCH, grid, PATCH).transpose(1, 3, 0, 2, 4)
    patches = patches.reshape(grid * grid, 3 * PATCH * PATCH).astype(jnp.bfloat16)
    hidden = jnp.dot(patches, patch_weight, preferred_element_type=jnp.float32)
    embed = jnp.dot(time_embedding(step_time, TEMB)[None, :], time_weight, preferred_element_type=jnp.float32)[0]
    time_scale = embed[:CH]
    time_shift = embed[CH:]
    first = jax.nn.silu(group_norm(hidden)).astype(jnp.bfloat16)
    inner = convolve(first.reshape(grid, grid, CH), conv_first)
    second = jax.nn.silu(group_norm(inner) * (1.0 + time_scale) + time_shift).astype(jnp.bfloat16)
    block = hidden + convolve(second.reshape(grid, grid, CH), conv_second)
    normed = group_norm(block).astype(jnp.bfloat16)
    projected = jnp.dot(normed, attn_weight, preferred_element_type=jnp.float32).astype(jnp.bfloat16)
    queries = projected[:, :CH].reshape(-1, HEADS, HEAD_DIM).astype(jnp.float32)
    keys = projected[:, CH:2 * CH].reshape(-1, HEADS, HEAD_DIM).astype(jnp.float32)
    values = projected[:, 2 * CH:].reshape(-1, HEADS, HEAD_DIM).astype(jnp.float32)
    scores = jnp.einsum('qhd,khd->hqk', queries, keys) / math.sqrt(HEAD_DIM)
    weights = jax.nn.softmax(scores, axis=-1).astype(jnp.bfloat16)
    attended = jnp.einsum('hqk,khd->qhd', weights.astype(jnp.float32), values)
    attended = attended.reshape(-1, CH).astype(jnp.bfloat16)
    mixed = block + jnp.dot(attended, proj_weight, preferred_element_type=jnp.float32)
    predicted = jnp.dot(mixed.astype(jnp.bfloat16), out_weight, preferred_element_type=jnp.float32)
    predicted = predicted.reshape(grid, grid, 3, PATCH, PATCH).transpose(2, 0, 3, 1, 4)
    return predicted.reshape(3, grid * PATCH, grid * PATCH)

def reference(states, noise_field, window_start, patch_weight, time_weight, conv_first, conv_second, attn_weight, proj_weight, out_weight):
    step_times = (999 - window_start[0] - jnp.arange(STEPS, dtype=jnp.int32)).astype(jnp.int32)

    def one_step(items):
        field, noise_now, step_time = items
        beta_now, keep_bar = plan(step_time)
        retain = 1.0 - beta_now
        predicted = denoiser(field, step_time, patch_weight, time_weight, conv_first, conv_second, attn_weight, proj_weight, out_weight)
        return (lax.rsqrt(retain) - 1.0) * field - beta_now * lax.rsqrt(retain) * lax.rsqrt(1.0 - keep_bar) * predicted + jnp.sqrt(beta_now) * noise_now
    drifts = lax.map(one_step, (states, noise_field, step_times))
    return states[0][None] + jnp.cumsum(drifts, axis=0)
```

```python
import math

import jax
import jax.numpy as jnp
from jax import lax
from jax.experimental import pallas as pl
from jax.experimental.pallas import tpu as pltpu
from jax.sharding import PartitionSpec as P

CH = 512
HEADS = 8
PATCH = 8
TEMB = 128
FEAT = 192
GRID = 32
ROWS = 256
EDGE = 32
ALL = ROWS + 2 * EDGE
PLANE = 8
LINES = 8
QUADS = 4
EPS = 1e-05
MESH = pl.DeviceIdType.MESH
F32 = jnp.float32
BF16 = jnp.bfloat16
NT = (((1,), (1,)), ((), ()))


def iota(shape, dim):
    return lax.broadcasted_iota(jnp.int32, shape, dim)


def dot(a, b):
    return jnp.dot(a, b, preferred_element_type=F32)


def dot_nt(a, b):
    return lax.dot_general(a, b, NT, preferred_element_type=F32)


def pack(x):
    low = jnp.concatenate([x[16:24, :128], x[16:24, 128:]], axis=0)
    return jnp.concatenate([x[:16], low], axis=1).astype(BF16)


def unpack(y):
    y = y.astype(F32)
    low = jnp.concatenate([y[:8, 256:], y[8:, 256:]], axis=1)
    return jnp.concatenate([y[:, :256], low], axis=0)


def sums_of(x):
    def fold(v):
        v = jnp.sum(v, axis=0, keepdims=True)
        return [v[:, 128 * i : 128 * (i + 1)] for i in range(4)]

    return jnp.concatenate(fold(x) + fold(x * x), axis=0)


def scale_shift(total, count):
    lane = iota((8, 128), 1)
    for s in (1, 2, 4, 8):
        up = pltpu.roll(total, 128 - s, axis=1)
        down = pltpu.roll(total, s, axis=1)
        total = total + jnp.where((lane & s) == 0, up, down)
    total = total / count
    mean, square = total[:4], total[4:]
    rstd = lax.rsqrt(square - mean * mean + EPS)
    shift = -mean * rstd

    def flat(v):
        return jnp.concatenate([v[i : i + 1] for i in range(4)], axis=1)

    return flat(rstd), flat(shift)


def kernel(
    st_h, no_h, ws, pw_h, tw_h, c1_h, c2_h, aw_h, pr_h, ow_h, out,
    st, no, pw, tw, c1, c2, aw, pr, ow, wqt, wvt, prt, owt,
    hid, act, inn, blk, blkt, nrm, kbuf, vbuf, qz, att, mref, lref, big,
    stat_own, stat_in, e_own, e_in, e_tot, e_line, e_pre, e_out,
    p_own, p_in, p_tot, p_line, p_pre, p_out,
    load, halo_s, halo_r, stat_s, stat_r, inn_s, inn_r, gat_s, gat_r,
    ea_s, ea_r, eb_s, eb_r, ec_s, ec_r, pa_s, pa_r, pb_s, pb_r, pc_s, pc_r,
):
    step = lax.axis_index("step")
    quad = lax.axis_index("quad")
    line = step // PLANE
    spot = step % PLANE

    loads = [
        pltpu.make_async_copy(st_h, st.at[:, pl.ds(8, 64), :], load.at[0]),
        pltpu.make_async_copy(pw_h, pw, load.at[1]),
        pltpu.make_async_copy(no_h, no, load.at[2]),
        pltpu.make_async_copy(tw_h, tw, load.at[3]),
        pltpu.make_async_copy(c1_h, c1, load.at[4]),
        pltpu.make_async_copy(c2_h, c2, load.at[5]),
        pltpu.make_async_copy(aw_h, aw, load.at[6]),
        pltpu.make_async_copy(pr_h, pr, load.at[7]),
        pltpu.make_async_copy(ow_h, ow, load.at[8]),
    ]
    for item in loads:
        item.start()

    def at_quad(j):
        return (step, (quad + j) % QUADS)

    def at_spot(j):
        return (line * PLANE + (spot + j) % PLANE, quad)

    def at_line(j):
        return (((line + j) % LINES) * PLANE + spot, quad)

    barrier = pltpu.get_barrier_semaphore()
    peers = [at_quad(j) for j in range(1, QUADS)]
    peers += [at_spot(j) for j in range(1, PLANE)]
    peers += [at_line(j) for j in range(1, LINES)]
    for peer in peers:
        pl.semaphore_signal(barrier, inc=1, device_id=peer, device_id_type=MESH)
    pl.semaphore_wait(barrier, len(peers))

    def send(src, dst, ss, rs, peer):
        copy = pltpu.make_async_remote_copy(
            src_ref=src, dst_ref=dst, send_sem=ss, recv_sem=rs, device_id=peer, device_id_type=MESH
        )
        copy.start()
        return copy

    loads[0].wait()
    halo = [
        send(st.at[:, pl.ds(64, 8), :], st.at[:, pl.ds(0, 8), :], halo_s.at[0], halo_r.at[0], at_quad(1)),
        send(st.at[:, pl.ds(8, 8), :], st.at[:, pl.ds(72, 8), :], halo_s.at[1], halo_r.at[1], at_quad(3)),
    ]

    feat = iota((FEAT, ROWS), 0)
    pixel = iota((FEAT, ROWS), 1)
    diag = (feat & 7) == (pixel & 7)
    spread = (iota((FEAT, 24), 0) >> 3 == iota((FEAT, 24), 1)).astype(F32).astype(BF16)
    gather = (iota((GRID, ROWS), 0) == iota((GRID, ROWS), 1) >> 3).astype(F32).astype(BF16)

    def embed_row(r):
        rows = st[:, pl.ds(pl.multiple_of(8 * r, 8), 8), :].reshape(24, ROWS).astype(BF16)
        wide = jnp.where(diag, dot(spread, rows), 0.0).astype(BF16)
        patches = dot_nt(gather, wide).astype(BF16)
        hid[pl.ds(pl.multiple_of(GRID * r, GRID), GRID), :] = dot(patches, pw[...])

    loads[1].wait()

    @pl.loop(1, 9)
    def _(r):
        embed_row(r)

    own = pl.ds(EDGE, ROWS)

    def share_sums(k, x):
        stat_own[k] = sums_of(x)
        return [
            send(stat_own.at[k], stat_in.at[k, j - 1], stat_s.at[3 * k + j - 1], stat_r.at[3 * k + j - 1], at_quad(j))
            for j in range(1, QUADS)
        ]

    def total_sums(k, copies):
        total = stat_own[k]
        for j, copy in enumerate(copies):
            copy.wait()
            total = total + stat_in[k, j]
        return scale_shift(total, float(QUADS * ROWS * CH // 32))

    stats = share_sums(0, hid[own, :])

    time = 999 - ws[0] - step
    when = jnp.full((8, 128), time.astype(F32))
    place = iota((8, 128), 0) * 128 + iota((8, 128), 1)
    beta_all = 0.0001 + (0.02 - 0.0001) * place.astype(F32) / 999.0
    log_all = jnp.where(place <= time, jnp.log1p(-beta_all), 0.0)
    log_now = jnp.sum(jnp.sum(log_all, axis=1, keepdims=True), axis=0, keepdims=True)
    beta = (0.0001 + (0.02 - 0.0001) * when / 999.0)[:1, :1]
    keep = jnp.exp(log_now)
    root = lax.rsqrt(1.0 - beta)
    of_state = root - 1.0
    of_noise = jnp.sqrt(beta)
    of_pred = -beta * root * lax.rsqrt(1.0 - keep)
    half = TEMB // 2
    lane = iota((8, TEMB), 1)
    angle = when * jnp.exp(-math.log(10000.0) * (lane & (half - 1)).astype(F32) / half)
    embed = jnp.where(lane < half, jnp.cos(angle), jnp.sin(angle)).astype(BF16)
    loads[3].wait()
    embed = dot(embed, tw[...])[:1]
    time_scale, time_shift = 1.0 + embed[:, :CH], embed[:, CH:]

    loads[2].wait()
    head = jnp.where(step == 0, 1.0, 0.0)

    @pl.loop(0, 8)
    def _(r):
        here = st[:, pl.ds(pl.multiple_of(8 * r + 8, 8), 8), :].reshape(24, ROWS)
        push = no[:, pl.ds(pl.multiple_of(8 * r, 8), 8), :].reshape(24, ROWS)
        e_own[r] = (of_state + head) * here + of_noise * push

    def scatter(own_ref, in_ref, ss, rs):
        return [
            send(own_ref.at[(spot + j) % PLANE], in_ref.at[spot], ss.at[j], rs.at[j], at_spot(j))
            for j in range(1, PLANE)
        ]

    def to_lines(tot, line_in, ss, rs, start):
        for j in range(1, LINES):
            copy = pltpu.make_async_remote_copy(
                src_ref=tot, dst_ref=line_in.at[j], send_sem=ss.at[j], recv_sem=rs.at[j],
                device_id=at_line(j), device_id_type=MESH,
            )

            @pl.when(line + j < LINES)
            def _():
                if start:
                    copy.start()
                else:
                    copy.wait_send()

            if not start:

                @pl.when(line >= j)
                def _():
                    copy.wait_recv()

    def lines_sum(line_in, shape, load_one):
        base = jnp.zeros(shape, F32)
        for j in range(1, LINES):
            base = base + jnp.where(line >= j, load_one(line_in, j), 0.0)
        return base

    def back(pre, out_ref, ss, rs):
        return [
            send(pre.at[(spot + j) % PLANE], out_ref.at[spot], ss.at[j], rs.at[j], at_spot(j))
            for j in range(1, PLANE)
        ]

    early_a = scatter(e_own, e_in, ea_s, ea_r)

    for item in halo:
        item.wait()
    embed_row(0)
    embed_row(9)
    scale, shift = total_sums(0, stats)

    def activate(source, gain, bias):
        @pl.loop(0, 10)
        def _(r):
            where = pl.ds(pl.multiple_of(GRID * r, GRID), GRID)
            x = source[where, :] * gain + bias
            outside = ((quad == 0) & (r == 0)) | ((quad == QUADS - 1) & (r == 9))
            x = x * (jnp.tanh(0.5 * x) + 1.0) * jnp.where(outside, 0.0, 0.5)
            col = iota((GRID, CH), 0)
            act[0, where, :] = jnp.where(col == 0, 0.0, pltpu.roll(x, 1, axis=0)).astype(BF16)
            act[1, where, :] = x.astype(BF16)
            act[2, where, :] = jnp.where(col == GRID - 1, 0.0, pltpu.roll(x, GRID - 1, axis=0)).astype(BF16)

    def convolve(weight, n):
        total = None
        for row in range(3):
            for col in range(3):
                term = dot(
                    act[col, pl.ds(GRID * row, ROWS), :],
                    weight[pl.ds((3 * row + col) * CH, CH), pl.ds(256 * n, 256)],
                )
                total = term if total is None else total + term
        return total

    activate(hid, scale, shift)
    loads[4].wait()
    for n in range(2):
        inn[own, pl.ds(256 * n, 256)] = convolve(c1, n)
    edges = [
        send(inn.at[pl.ds(ROWS, EDGE)], inn.at[pl.ds(0, EDGE)], inn_s.at[0], inn_r.at[0], at_quad(1)),
        send(inn.at[pl.ds(EDGE, EDGE)], inn.at[pl.ds(ALL - EDGE, EDGE)], inn_s.at[1], inn_r.at[1], at_quad(3)),
    ]
    stats = share_sums(1, inn[own, :])

    for item in early_a:
        item.wait()
    e_in[spot] = e_own[spot]
    run = jnp.zeros((24, ROWS), F32)
    for d in range(PLANE):
        e_pre[d] = run
        run = run + e_in[d]
    e_tot[...] = run
    to_lines(e_tot, e_line, eb_s, eb_r, True)
    loads[6].wait()
    wqt[...] = aw[:, :CH].T

    for item in edges:
        item.wait()
    scale, shift = total_sums(1, stats)
    activate(inn, scale * time_scale, shift * time_scale + time_shift)
    loads[5].wait()
    for n in range(2):
        lanes = pl.ds(256 * n, 256)
        blk[:, lanes] = hid[own, lanes] + convolve(c2, n)
    stats = share_sums(2, blk[...])

    to_lines(e_tot, e_line, eb_s, eb_r, False)
    base = lines_sum(e_line, (24, ROWS), lambda ref, j: ref[j])
    for d in range(PLANE):
        e_pre[d] = e_pre[d] + base
    early_c = back(e_pre, e_out, ec_s, ec_r)
    wvt[...] = aw[:, 2 * CH :].T

    scale, shift = total_sums(2, stats)
    nrm[0] = (blk[...] * scale + shift).astype(BF16)
    low, high = pl.ds(0, 128), pl.ds(128, 128)
    low_r = send(nrm.at[0, low], nrm.at[1, low], gat_s.at[0], gat_r.at[0], at_quad(1))
    high_l = send(nrm.at[0, high], nrm.at[2, high], gat_s.at[1], gat_r.at[1], at_quad(3))
    high_r = send(nrm.at[0, high], nrm.at[1, high], gat_s.at[2], gat_r.at[2], at_quad(1))
    low_l = send(nrm.at[0, low], nrm.at[2, low], gat_s.at[3], gat_r.at[3], at_quad(3))

    queries = dot_nt(wqt[...], nrm[0]).astype(BF16)
    upper = iota((128, ROWS), 0) < 64
    for p in range(4):
        pair = queries[128 * p : 128 * (p + 1)]
        qz[2 * p] = jnp.where(upper, pair, jnp.zeros_like(pair))
        qz[2 * p + 1] = jnp.where(upper, jnp.zeros_like(pair), pair)
    sharp = math.log2(math.e) / 8.0

    def attend(slot):
        normed = nrm[slot]
        kbuf[...] = dot(normed, aw[:, CH : 2 * CH]).astype(BF16)
        vbuf[...] = dot_nt(wvt[...], normed).astype(BF16)

        @pl.loop(0, 4)
        def _(p):
            keys = kbuf[:, pl.ds(pl.multiple_of(128 * p, 128), 128)]
            for side in range(2):
                h = 2 * p + side
                rows = pl.ds(pl.multiple_of(64 * h, 64), 64)
                scores = dot(keys, qz[h])
                most = jnp.max(scores, axis=0, keepdims=True)
                if slot > 0:
                    most = jnp.maximum(most, mref[h])
                weights = jnp.exp2((scores - most) * sharp)
                total = jnp.sum(weights, axis=0, keepdims=True)
                value = dot(vbuf[rows, :], weights.astype(BF16))
                if slot > 0:
                    fade = jnp.exp2((mref[h] - most) * sharp)
                    total = total + lref[h] * fade
                    value = value + att[rows, :] * fade
                mref[h] = most
                lref[h] = total
                att[rows, :] = value

    attend(0)
    low_r.wait_recv()
    pass_r = send(nrm.at[1, low], nrm.at[3, low], gat_s.at[4], gat_r.at[4], at_quad(1))
    high_l.wait_recv()
    pass_l = send(nrm.at[2, high], nrm.at[3, high], gat_s.at[5], gat_r.at[5], at_quad(3))
    loads[7].wait()
    loads[8].wait()
    prt[...] = pr[...].T
    owt[...] = ow[...].T
    blkt[...] = blk[...].T
    big[...] = (iota((ROWS, 8 * ROWS), 0) == iota((ROWS, 8 * ROWS), 1) >> 3).astype(F32).astype(BF16)
    high_r.wait_recv()
    attend(1)
    low_l.wait_recv()
    attend(2)
    pass_r.wait_recv()
    pass_l.wait_recv()
    attend(3)
    for h in range(HEADS):
        rows = pl.ds(64 * h, 64)
        att[rows, :] = att[rows, :] / lref[h]

    mixed = blkt[...] + dot(prt[...], att[...].astype(BF16))
    predicted = (dot(owt[...], mixed.astype(BF16)) * of_pred).astype(BF16)
    for r in range(8):
        wide = dot(predicted, big[:, 256 * r : 256 * (r + 1)])
        wide = jnp.where(diag, wide, 0.0).astype(BF16)
        p_own[r] = pack(lax.dot_general(spread, wide, (((0,), (0,)), ((), ())), preferred_element_type=F32))

    late_a = scatter(p_own, p_in, pa_s, pa_r)
    p_in[spot] = p_own[spot]
    for item in late_a:
        item.wait()
    run = jnp.zeros((16, 384), F32)
    runs = []
    for d in range(PLANE):
        runs.append(run)
        run = run + p_in[d].astype(F32)
    p_tot[...] = run.astype(BF16)
    to_lines(p_tot, p_line, pb_s, pb_r, True)
    for item in early_c:
        item.wait()
    e_out[spot] = e_pre[spot]
    to_lines(p_tot, p_line, pb_s, pb_r, False)
    base = lines_sum(p_line, (16, 384), lambda ref, j: ref[j].astype(F32))
    for d in range(PLANE):
        p_pre[d] = (runs[d] + base).astype(BF16)
    late_c = back(p_pre, p_out, pc_s, pc_r)
    p_out[spot] = p_pre[spot]
    for item in late_c:
        item.wait()
    for r in range(8):
        late = unpack(p_out[r]) + unpack(p_own[r])
        out[:, pl.ds(8 * r, 8), :] = (e_out[r] + e_own[r] + late).reshape(3, 8, ROWS)
    for item in (low_r, high_l, high_r, low_l, pass_r, pass_l):
        item.wait_send()


def body(states, noise, ws, pw, tw, c1, c2, aw, pr, ow):
    dma = pltpu.SemaphoreType.DMA
    vmem = pltpu.VMEM
    anyhow = pl.BlockSpec(memory_space=pl.ANY)
    chunk, small = (24, ROWS), (16, 384)
    scratch = [
        vmem((3, 80, 256), F32), vmem((3, 64, 256), F32),
        vmem((FEAT, CH), BF16), vmem((TEMB, 2 * CH), BF16),
        vmem((9 * CH, CH), BF16), vmem((9 * CH, CH), BF16),
        vmem((CH, 3 * CH), BF16), vmem((CH, CH), BF16), vmem((CH, FEAT), BF16),
        vmem((CH, CH), BF16), vmem((CH, CH), BF16), vmem((CH, CH), BF16), vmem((FEAT, CH), BF16),
        vmem((ALL, CH), F32), vmem((3, ALL, CH), BF16), vmem((ALL, CH), F32),
        vmem((ROWS, CH), F32), vmem((CH, ROWS), F32),
        vmem((4, ROWS, CH), BF16), vmem((ROWS, CH), BF16), vmem((CH, ROWS), BF16),
        vmem((8, 128, ROWS), BF16), vmem((CH, ROWS), F32),
        vmem((8, 1, ROWS), F32), vmem((8, 1, ROWS), F32), vmem((ROWS, 8 * ROWS), BF16),
        vmem((3, 8, 128), F32), vmem((3, 3, 8, 128), F32),
        vmem((8,) + chunk, F32), vmem((8,) + chunk, F32), vmem(chunk, F32), vmem((8,) + chunk, F32),
        vmem((8,) + chunk, F32), vmem((8,) + chunk, F32),
        vmem((8,) + small, BF16), vmem((8,) + small, BF16), vmem(small, BF16), vmem((8,) + small, BF16),
        vmem((8,) + small, BF16), vmem((8,) + small, BF16),
        dma((9,)), dma((2,)), dma((2,)), dma((9,)), dma((9,)), dma((2,)), dma((2,)), dma((6,)), dma((6,)),
    ] + [dma((8,)) for _ in range(12)]
    result = pl.pallas_call(
        kernel,
        out_shape=jax.ShapeDtypeStruct((3, 64, 256), F32),
        in_specs=[anyhow, anyhow, pl.BlockSpec(memory_space=pltpu.SMEM)] + [anyhow] * 7,
        out_specs=pl.BlockSpec(memory_space=pltpu.VMEM),
        scratch_shapes=scratch,
        compiler_params=pltpu.CompilerParams(
            collective_id=0, has_side_effects=True, vmem_limit_bytes=56 * 1024 * 1024
        ),
    )(
        states[0], noise[0], ws, pw, tw,
        c1.reshape(9 * CH, CH), c2.reshape(9 * CH, CH), aw, pr, ow,
    )
    return result[None]


def solution(mesh):
    image = P("step", None, "quad", None)
    return jax.shard_map(
        body,
        mesh=mesh,
        in_specs=(image, image) + (P(),) * 8,
        out_specs=image,
        check_vma=False,
    )
```

```python
import math

import jax
import jax.numpy as jnp
from jax import lax
from jax.experimental import pallas as pl
from jax.experimental.pallas import tpu as pltpu
from jax.sharding import PartitionSpec as P

CH = 512
HEADS = 8
GROUP = 8
PATCH = 8
TEMB = 128
FEAT = 192
GRID = 32
ROWS = 256
EDGE = 32
ALL = ROWS + 2 * EDGE
PLANE = 8
LINES = 8
QUADS = 4
EPS = 1e-05
MESH = pl.DeviceIdType.MESH
F32 = jnp.float32
BF16 = jnp.bfloat16
NT = (((1,), (1,)), ((), ()))


def iota(shape, dim):
    return lax.broadcasted_iota(jnp.int32, shape, dim)


def dot(a, b):
    return jnp.dot(a, b, preferred_element_type=F32)


def dot_nt(a, b):
    return lax.dot_general(a, b, NT, preferred_element_type=F32)


def pack(x):
    low = jnp.concatenate([x[16:24, :128], x[16:24, 128:]], axis=0)
    return jnp.concatenate([x[:16], low], axis=1).astype(BF16)


def unpack(y):
    y = y.astype(F32)
    low = jnp.concatenate([y[:8, 256:], y[8:, 256:]], axis=1)
    return jnp.concatenate([y[:, :256], low], axis=0)


def sums_of(x):
    def fold(v):
        v = jnp.sum(v, axis=0, keepdims=True)
        return [v[:, 128 * i : 128 * (i + 1)] for i in range(4)]

    return jnp.concatenate(fold(x) + fold(x * x), axis=0)


def scale_shift(total, count):
    lane = iota((8, 128), 1)
    for s in (1, 2, 4, 8):
        up = pltpu.roll(total, 128 - s, axis=1)
        down = pltpu.roll(total, s, axis=1)
        total = total + jnp.where((lane & s) == 0, up, down)
    total = total / count
    mean, square = total[:4], total[4:]
    rstd = lax.rsqrt(square - mean * mean + EPS)
    shift = -mean * rstd

    def flat(v):
        return jnp.concatenate([v[i : i + 1] for i in range(4)], axis=1)

    return flat(rstd), flat(shift)


def kernel(
    st_h, no_h, ws, pw_h, tw_h, c1_h, c2_h, aw_h, pr_h, ow_h, out,
    st, no, pw, tw, c1, c2, aw, pr, ow, wqt, wvt, prt,
    hid, act, inn, blk, blkt, nrm, kbuf, vbuf, qz, att, mref, lref, big,
    stat_own, stat_in, e_own, e_in, e_tot, e_line, e_pre, e_out,
    p_own, p_in, p_tot, p_line, p_pre, p_out,
    load, halo_s, halo_r, stat_s, stat_r, inn_s, inn_r, gat_s, gat_r,
    ea_s, ea_r, eb_s, eb_r, ec_s, ec_r, pa_s, pa_r, pb_s, pb_r, pc_s, pc_r,
):
    step = lax.axis_index("step")
    quad = lax.axis_index("quad")
    line = step // PLANE
    spot = step % PLANE


    def at_quad(j):
        return (step, (quad + j) % QUADS)

    def at_spot(j):
        return (line * PLANE + (spot + j) % PLANE, quad)

    def at_line(j):
        return (((line + j) % LINES) * PLANE + spot, quad)

    barrier = pltpu.get_barrier_semaphore()
    peers = [at_line(j) for j in (4, 3, 5, 2, 6, 1, 7)]
    peers += [at_spot(j) for j in range(1, PLANE)]
    peers += [at_quad(j) for j in range(1, QUADS)]
    for peer in peers:
        pl.semaphore_signal(barrier, inc=1, device_id=peer, device_id_type=MESH)

    def send(src, dst, ss, rs, peer):
        copy = pltpu.make_async_remote_copy(
            src_ref=src, dst_ref=dst, send_sem=ss, recv_sem=rs, device_id=peer, device_id_type=MESH
        )
        copy.start()
        return copy

    loads = [
        pltpu.make_async_copy(st_h, st.at[:, pl.ds(8, 64), :], load.at[0]),
        pltpu.make_async_copy(pw_h, pw, load.at[1]),
        pltpu.make_async_copy(no_h, no, load.at[2]),
        pltpu.make_async_copy(tw_h, tw, load.at[3]),
        pltpu.make_async_copy(c1_h, c1, load.at[4]),
        pltpu.make_async_copy(c2_h, c2, load.at[5]),
        pltpu.make_async_copy(aw_h, aw, load.at[6]),
        pltpu.make_async_copy(pr_h, pr, load.at[7]),
        pltpu.make_async_copy(ow_h, ow, load.at[8]),
    ]
    for item in loads:
        item.start()
    feat = iota((FEAT, ROWS), 0)
    pixel = iota((FEAT, ROWS), 1)
    diag = (feat & 7) == (pixel & 7)
    spread = (iota((FEAT, 24), 0) >> 3 == iota((FEAT, 24), 1)).astype(F32).astype(BF16)
    gather = (iota((GRID, ROWS), 0) == iota((GRID, ROWS), 1) >> 3).astype(F32).astype(BF16)

    def embed_row(r):
        rows = st[:, pl.ds(pl.multiple_of(8 * r, 8), 8), :].reshape(24, ROWS).astype(BF16)
        wide = jnp.where(diag, dot(spread, rows), 0.0).astype(BF16)
        patches = dot_nt(gather, wide).astype(BF16)
        hid[pl.ds(pl.multiple_of(GRID * r, GRID), GRID), :] = dot(patches, pw[...])

    loads[0].wait()
    loads[1].wait()

    @pl.loop(1, 9)
    def _(r):
        embed_row(r)

    own = pl.ds(EDGE, ROWS)
    stat_own[0] = sums_of(hid[own, :])

    time = 999 - ws[0] - step
    when = jnp.full((8, 128), time.astype(F32))
    place = iota((8, 128), 0) * 128 + iota((8, 128), 1)
    beta_all = 0.0001 + (0.02 - 0.0001) * place.astype(F32) / 999.0
    log_all = jnp.where(place <= time, jnp.log1p(-beta_all), 0.0)
    log_now = jnp.sum(jnp.sum(log_all, axis=1, keepdims=True), axis=0, keepdims=True)
    beta = (0.0001 + (0.02 - 0.0001) * when / 999.0)[:1, :1]
    keep = jnp.exp(log_now)
    root = lax.rsqrt(1.0 - beta)
    of_state = root - 1.0
    of_noise = jnp.sqrt(beta)
    of_pred = -beta * root * lax.rsqrt(1.0 - keep)
    half = TEMB // 2
    lane = iota((8, TEMB), 1)
    angle = when * jnp.exp(-math.log(10000.0) * (lane & (half - 1)).astype(F32) / half)
    embed = jnp.where(lane < half, jnp.cos(angle), jnp.sin(angle)).astype(BF16)
    loads[3].wait()
    embed = dot(embed, tw[...])[:1]
    time_scale, time_shift = 1.0 + embed[:, :CH], embed[:, CH:]

    loads[2].wait()
    head = jnp.where(step == 0, 1.0, 0.0)

    @pl.loop(0, 8)
    def _(r):
        here = st[:, pl.ds(pl.multiple_of(8 * r + 8, 8), 8), :].reshape(24, ROWS)
        push = no[:, pl.ds(pl.multiple_of(8 * r, 8), 8), :].reshape(24, ROWS)
        e_own[r] = (of_state + head) * here + of_noise * push

    pl.semaphore_wait(barrier, len(peers))
    halo = [
        send(st.at[:, pl.ds(64, 8), :], st.at[:, pl.ds(0, 8), :], halo_s.at[0], halo_r.at[0], at_quad(1)),
        send(st.at[:, pl.ds(8, 8), :], st.at[:, pl.ds(72, 8), :], halo_s.at[1], halo_r.at[1], at_quad(3)),
    ]


    def share_sums(k):
        return [
            send(stat_own.at[k], stat_in.at[k, j - 1], stat_s.at[3 * k + j - 1], stat_r.at[3 * k + j - 1], at_quad(j))
            for j in range(1, QUADS)
        ]

    def total_sums(k, copies):
        total = stat_own[k]
        for j, copy in enumerate(copies):
            copy.wait()
            total = total + stat_in[k, j]
        return scale_shift(total, float(QUADS * ROWS * CH // 32))

    stats = share_sums(0)

    def scatter(own_ref, in_ref, ss, rs):
        return [
            send(own_ref.at[(spot + j) % PLANE], in_ref.at[spot], ss.at[j], rs.at[j], at_spot(j))
            for j in range(1, PLANE)
        ]

    def to_lines(tot, line_in, ss, rs, start):
        for j in range(1, LINES):
            copy = pltpu.make_async_remote_copy(
                src_ref=tot, dst_ref=line_in.at[j], send_sem=ss.at[j], recv_sem=rs.at[j],
                device_id=at_line(j), device_id_type=MESH,
            )

            @pl.when(line + j < LINES)
            def _():
                if start:
                    copy.start()
                else:
                    copy.wait_send()

            if not start:

                @pl.when(line >= j)
                def _():
                    copy.wait_recv()

    def lines_sum(line_in, shape, load_one):
        base = jnp.zeros(shape, F32)
        for j in range(1, LINES):
            base = base + jnp.where(line >= j, load_one(line_in, j), 0.0)
        return base

    def back(pre, out_ref, ss, rs):
        return [
            send(pre.at[(spot + j) % PLANE], out_ref.at[spot], ss.at[j], rs.at[j], at_spot(j))
            for j in range(1, PLANE)
        ]

    early_a = scatter(e_own, e_in, ea_s, ea_r)

    for item in halo:
        item.wait()
    embed_row(0)
    embed_row(9)
    scale, shift = total_sums(0, stats)

    def activate(source, gain, bias):
        @pl.loop(0, 10)
        def _(r):
            where = pl.ds(pl.multiple_of(GRID * r, GRID), GRID)
            x = source[where, :] * gain + bias
            outside = ((quad == 0) & (r == 0)) | ((quad == QUADS - 1) & (r == 9))
            x = x * (jnp.tanh(0.5 * x) + 1.0) * jnp.where(outside, 0.0, 0.5)
            col = iota((GRID, CH), 0)
            act[0, where, :] = jnp.where(col == 0, 0.0, pltpu.roll(x, 1, axis=0)).astype(BF16)
            act[1, where, :] = x.astype(BF16)
            act[2, where, :] = jnp.where(col == GRID - 1, 0.0, pltpu.roll(x, GRID - 1, axis=0)).astype(BF16)

    def convolve(weight, n):
        total = None
        for row in range(3):
            for col in range(3):
                term = dot(
                    act[col, pl.ds(GRID * row, ROWS), :],
                    weight[pl.ds((3 * row + col) * CH, CH), pl.ds(256 * n, 256)],
                )
                total = term if total is None else total + term
        return total

    activate(hid, scale, shift)
    loads[4].wait()
    for n in range(2):
        inn[own, pl.ds(256 * n, 256)] = convolve(c1, n)
    edges = [
        send(inn.at[pl.ds(ROWS, EDGE)], inn.at[pl.ds(0, EDGE)], inn_s.at[0], inn_r.at[0], at_quad(1)),
        send(inn.at[pl.ds(EDGE, EDGE)], inn.at[pl.ds(ALL - EDGE, EDGE)], inn_s.at[1], inn_r.at[1], at_quad(3)),
    ]
    stat_own[1] = sums_of(inn[own, :])
    stats = share_sums(1)

    for item in early_a:
        item.wait()
    e_in[spot] = e_own[spot]
    run = jnp.zeros((24, ROWS), F32)
    for d in range(PLANE):
        e_pre[d] = run
        run = run + e_in[d]
    e_tot[...] = run
    to_lines(e_tot, e_line, eb_s, eb_r, True)
    loads[6].wait()
    wqt[...] = aw[:, :CH].T

    for item in edges:
        item.wait()
    scale, shift = total_sums(1, stats)
    activate(inn, scale * time_scale, shift * time_scale + time_shift)
    loads[5].wait()
    for n in range(2):
        lanes = pl.ds(256 * n, 256)
        blk[:, lanes] = hid[own, lanes] + convolve(c2, n)
    stat_own[2] = sums_of(blk[...])
    stats = share_sums(2)

    to_lines(e_tot, e_line, eb_s, eb_r, False)
    base = lines_sum(e_line, (24, ROWS), lambda ref, j: ref[j])
    for d in range(PLANE):
        e_pre[d] = e_pre[d] + base
    early_c = back(e_pre, e_out, ec_s, ec_r)
    wvt[...] = aw[:, 2 * CH :].T

    scale, shift = total_sums(2, stats)
    nrm[0] = (blk[...] * scale + shift).astype(BF16)
    low, high = pl.ds(0, 128), pl.ds(128, 128)
    low_r = send(nrm.at[0, low], nrm.at[1, low], gat_s.at[0], gat_r.at[0], at_quad(1))
    high_l = send(nrm.at[0, high], nrm.at[2, high], gat_s.at[1], gat_r.at[1], at_quad(3))
    high_r = send(nrm.at[0, high], nrm.at[1, high], gat_s.at[2], gat_r.at[2], at_quad(1))
    low_l = send(nrm.at[0, low], nrm.at[2, low], gat_s.at[3], gat_r.at[3], at_quad(3))

    queries = dot_nt(wqt[...], nrm[0]).astype(BF16)
    upper = iota((128, ROWS), 0) < 64
    for p in range(4):
        pair = queries[128 * p : 128 * (p + 1)]
        qz[2 * p] = jnp.where(upper, pair, jnp.zeros_like(pair))
        qz[2 * p + 1] = jnp.where(upper, jnp.zeros_like(pair), pair)
    sharp = math.log2(math.e) / 8.0

    def attend(slot):
        normed = nrm[slot]
        kbuf[...] = dot(normed, aw[:, CH : 2 * CH]).astype(BF16)
        vbuf[...] = dot_nt(wvt[...], normed).astype(BF16)

        def some(base):
            scores, most, weights, total = {}, {}, {}, {}
            for g in range(GROUP):
                h = base + g
                pair = pl.ds(pl.multiple_of(128 * (h // 2), 128), 128)
                scores[g] = dot(kbuf[:, pair], qz[h])
            for g in range(GROUP):
                h = base + g
                most[g] = jnp.max(scores[g], axis=0, keepdims=True)
                if slot > 0:
                    most[g] = jnp.maximum(most[g], mref[h])
                e = jnp.exp2((scores[g] - most[g]) * sharp)
                total[g] = jnp.sum(e, axis=0, keepdims=True)
                weights[g] = e.astype(BF16)
            for g in range(GROUP):
                h = base + g
                rows = pl.ds(pl.multiple_of(64 * h, 64), 64)
                value = dot(vbuf[rows, :], weights[g])
                if slot > 0:
                    fade = jnp.exp2((mref[h] - most[g]) * sharp)
                    total[g] = total[g] + lref[h] * fade
                    value = value + att[rows, :] * fade
                mref[h] = most[g]
                lref[h] = total[g]
                att[rows, :] = value

        if GROUP == HEADS:
            some(0)
        else:
            pl.loop(0, HEADS // GROUP)(lambda i: some(i * GROUP))

    attend(0)
    low_r.wait_recv()
    pass_r = send(nrm.at[1, low], nrm.at[3, low], gat_s.at[4], gat_r.at[4], at_quad(1))
    high_l.wait_recv()
    pass_l = send(nrm.at[2, high], nrm.at[3, high], gat_s.at[5], gat_r.at[5], at_quad(3))
    loads[7].wait()
    loads[8].wait()
    prt[...] = pr[...].T
    blkt[...] = blk[...].T
    big[...] = (iota((ROWS, 8 * ROWS), 0) == iota((ROWS, 8 * ROWS), 1) >> 3).astype(F32).astype(BF16)
    high_r.wait_recv()
    attend(1)
    low_l.wait_recv()
    attend(2)
    pass_r.wait_recv()
    pass_l.wait_recv()
    attend(3)
    for h in range(HEADS):
        rows = pl.ds(64 * h, 64)
        att[rows, :] = att[rows, :] / lref[h]

    mixed = blkt[...] + dot(prt[...], att[...].astype(BF16))
    predicted = (dot(ow[...], mixed.astype(BF16)) * of_pred).astype(BF16)
    for r in range(8):
        wide = dot(predicted, big[:, 256 * r : 256 * (r + 1)])
        wide = jnp.where(diag, wide, 0.0).astype(BF16)
        p_own[r] = pack(lax.dot_general(spread, wide, (((0,), (0,)), ((), ())), preferred_element_type=F32))

    late_a = scatter(p_own, p_in, pa_s, pa_r)
    p_in[spot] = p_own[spot]
    for item in late_a:
        item.wait()
    run = jnp.zeros((16, 384), F32)
    runs = []
    for d in range(PLANE):
        runs.append(run)
        run = run + p_in[d].astype(F32)
    p_tot[...] = run.astype(BF16)
    to_lines(p_tot, p_line, pb_s, pb_r, True)
    for item in early_c:
        item.wait()
    e_out[spot] = e_pre[spot]
    to_lines(p_tot, p_line, pb_s, pb_r, False)
    base = lines_sum(p_line, (16, 384), lambda ref, j: ref[j].astype(F32))
    for d in range(PLANE):
        p_pre[d] = (runs[d] + base).astype(BF16)
    late_c = back(p_pre, p_out, pc_s, pc_r)
    p_out[spot] = p_pre[spot]
    for item in late_c:
        item.wait()
    for r in range(8):
        late = unpack(p_out[r]) + unpack(p_own[r])
        out[:, pl.ds(8 * r, 8), :] = (e_out[r] + e_own[r] + late).reshape(3, 8, ROWS)
    for item in (low_r, high_l, high_r, low_l, pass_r, pass_l):
        item.wait_send()


def body(states, noise, ws, pw, tw, c1, c2, aw, pr, ow):
    dma = pltpu.SemaphoreType.DMA
    vmem = pltpu.VMEM
    anyhow = pl.BlockSpec(memory_space=pl.ANY)
    chunk, small = (24, ROWS), (16, 384)
    scratch = [
        vmem((3, 80, 256), F32), vmem((3, 64, 256), F32),
        vmem((FEAT, CH), BF16), vmem((TEMB, 2 * CH), BF16),
        vmem((9 * CH, CH), BF16), vmem((9 * CH, CH), BF16),
        vmem((CH, 3 * CH), BF16), vmem((CH, CH), BF16), vmem((FEAT, CH), BF16),
        vmem((CH, CH), BF16), vmem((CH, CH), BF16), vmem((CH, CH), BF16),
        vmem((ALL, CH), F32), vmem((3, ALL, CH), BF16), vmem((ALL, CH), F32),
        vmem((ROWS, CH), F32), vmem((CH, ROWS), F32),
        vmem((4, ROWS, CH), BF16), vmem((ROWS, CH), BF16), vmem((CH, ROWS), BF16),
        vmem((8, 128, ROWS), BF16), vmem((CH, ROWS), F32),
        vmem((8, 1, ROWS), F32), vmem((8, 1, ROWS), F32), vmem((ROWS, 8 * ROWS), BF16),
        vmem((3, 8, 128), F32), vmem((3, 3, 8, 128), F32),
        vmem((8,) + chunk, F32), vmem((8,) + chunk, F32), vmem(chunk, F32), vmem((8,) + chunk, F32),
        vmem((8,) + chunk, F32), vmem((8,) + chunk, F32),
        vmem((8,) + small, BF16), vmem((8,) + small, BF16), vmem(small, BF16), vmem((8,) + small, BF16),
        vmem((8,) + small, BF16), vmem((8,) + small, BF16),
        dma((9,)), dma((2,)), dma((2,)), dma((9,)), dma((9,)), dma((2,)), dma((2,)), dma((6,)), dma((6,)),
    ] + [dma((8,)) for _ in range(12)]
    result = pl.pallas_call(
        kernel,
        out_shape=jax.ShapeDtypeStruct((3, 64, 256), F32),
        in_specs=[anyhow, anyhow, pl.BlockSpec(memory_space=pltpu.SMEM)] + [anyhow] * 7,
        out_specs=pl.BlockSpec(memory_space=pltpu.VMEM),
        scratch_shapes=scratch,
        compiler_params=pltpu.CompilerParams(
            collective_id=0, has_side_effects=True, vmem_limit_bytes=56 * 1024 * 1024
        ),
    )(
        states[0], noise[0], ws, pw, tw,
        c1.reshape(9 * CH, CH), c2.reshape(9 * CH, CH), aw, pr, ow.T,
    )
    return result[None]


def solution(mesh):
    image = P("step", None, "quad", None)
    return jax.shard_map(
        body,
        mesh=mesh,
        in_specs=(image, image) + (P(),) * 8,
        out_specs=image,
        check_vma=False,
    )
```

```python
import math

import jax
import jax.numpy as jnp
from jax import lax
from jax.experimental import pallas as pl
from jax.experimental.pallas import tpu as pltpu
from jax.sharding import PartitionSpec as P

CH = 512
HEADS = 8
GROUP = 8
FAR = (5, 4, 3, 7, 2, 6, 1)
PATCH = 8
TEMB = 128
FEAT = 192
GRID = 32
ROWS = 256
EDGE = 32
ALL = ROWS + 2 * EDGE
PLANE = 8
LINES = 8
QUADS = 4
EPS = 1e-05
MESH = pl.DeviceIdType.MESH
F32 = jnp.float32
BF16 = jnp.bfloat16
NT = (((1,), (1,)), ((), ()))


def iota(shape, dim):
    return lax.broadcasted_iota(jnp.int32, shape, dim)


def dot(a, b):
    return jnp.dot(a, b, preferred_element_type=F32)


def dot_nt(a, b):
    return lax.dot_general(a, b, NT, preferred_element_type=F32)


def pack(x):
    low = jnp.concatenate([x[16:24, :128], x[16:24, 128:]], axis=0)
    return jnp.concatenate([x[:16], low], axis=1).astype(BF16)


def unpack(y):
    y = y.astype(F32)
    low = jnp.concatenate([y[:8, 256:], y[8:, 256:]], axis=1)
    return jnp.concatenate([y[:, :256], low], axis=0)


def flat(v):
    return jnp.concatenate([v[i : i + 1] for i in range(4)], axis=1)


def sums_of(x):
    def fold(v):
        v = jnp.sum(v, axis=0, keepdims=True)
        return [v[:, 128 * i : 128 * (i + 1)] for i in range(4)]

    return jnp.concatenate(fold(x) + fold(x * x), axis=0)


def scale_shift(total, count):
    lane = iota((8, 128), 1)
    for s in (1, 2, 4, 8):
        up = pltpu.roll(total, 128 - s, axis=1)
        down = pltpu.roll(total, s, axis=1)
        total = total + jnp.where((lane & s) == 0, up, down)
    total = total / count
    mean, square = total[:4], total[4:]
    rstd = lax.rsqrt(square - mean * mean + EPS)
    shift = -mean * rstd
    return flat(rstd), flat(shift)


def kernel(
    st_h, no_h, ws, pw_h, tw_h, c1_h, c2_h, aw_h, pr_h, ow_h, early, late,
    st, no, pw, tw, c1, c2, aw, pr, ow, wqt, wvt, prt,
    hid, act, inn, blk, blkt, kbuf, vbuf, qz, att, mref, lref, big,
    stat_own, stat_in, e_own, e_in, e_tot, e_line, e_pre, e_out, e_sum, ihalo, raw,
    p_own, p_in, p_tot, p_line, p_pre, p_out,
    load, early_sem, halo_s, halo_r, stat_s, stat_r, inn_s, inn_r, gat_s, gat_r,
    ea_s, ea_r, eb_s, eb_r, ec_s, ec_r, pa_s, pa_r, pb_s, pb_r, pc_s, pc_r,
):
    step = lax.axis_index("step")
    quad = lax.axis_index("quad")
    line = step // PLANE
    spot = step % PLANE


    def at_quad(j):
        return (step, (quad + j) % QUADS)

    def spot_of(j):
        return ((spot // 2 + j // 2) % 4) * 2 + (spot + j) % 2

    def at_spot(j):
        return (line * PLANE + spot_of(j), quad)

    def at_line(j):
        return (((line + j) % LINES) * PLANE + spot, quad)

    barrier = pltpu.get_barrier_semaphore()
    peers = [at_line(j) for j in (4, 3, 5, 2, 6, 1, 7)]
    peers += [at_spot(j) for j in FAR]
    peers += [at_quad(j) for j in range(1, QUADS)]
    for peer in peers:
        pl.semaphore_signal(barrier, inc=1, device_id=peer, device_id_type=MESH)

    def send(src, dst, ss, rs, peer):
        copy = pltpu.make_async_remote_copy(
            src_ref=src, dst_ref=dst, send_sem=ss, recv_sem=rs, device_id=peer, device_id_type=MESH
        )
        copy.start()
        return copy

    loads = [
        pltpu.make_async_copy(st_h, st.at[:, pl.ds(8, 64), :], load.at[0]),
        pltpu.make_async_copy(pw_h, pw, load.at[1]),
        pltpu.make_async_copy(no_h, no, load.at[2]),
        pltpu.make_async_copy(tw_h, tw, load.at[3]),
        pltpu.make_async_copy(c1_h, c1, load.at[4]),
        pltpu.make_async_copy(c2_h, c2, load.at[5]),
        pltpu.make_async_copy(aw_h, aw, load.at[6]),
        pltpu.make_async_copy(pr_h, pr, load.at[7]),
        pltpu.make_async_copy(ow_h, ow, load.at[8]),
    ]
    for item in loads:
        item.start()
    feat = iota((FEAT, ROWS), 0)
    pixel = iota((FEAT, ROWS), 1)
    diag = (feat & 7) == (pixel & 7)
    spread = (iota((FEAT, 24), 0) >> 3 == iota((FEAT, 24), 1)).astype(F32).astype(BF16)
    gather = (iota((GRID, ROWS), 0) == iota((GRID, ROWS), 1) >> 3).astype(F32).astype(BF16)

    def embed_row(r):
        rows = st[:, pl.ds(pl.multiple_of(8 * r, 8), 8), :].reshape(24, ROWS).astype(BF16)
        wide = jnp.where(diag, dot(spread, rows), 0.0).astype(BF16)
        patches = dot_nt(gather, wide).astype(BF16)
        hid[pl.ds(pl.multiple_of(GRID * r, GRID), GRID), :] = dot(patches, pw[...])

    loads[0].wait()
    loads[1].wait()

    @pl.loop(1, 9)
    def _(r):
        embed_row(r)

    own = pl.ds(EDGE, ROWS)
    stat_own[0] = sums_of(hid[own, :])

    time = 999 - ws[0] - step
    when = jnp.full((8, 128), time.astype(F32))
    place = iota((8, 128), 0) * 128 + iota((8, 128), 1)
    beta_all = 0.0001 + (0.02 - 0.0001) * place.astype(F32) / 999.0
    log_all = jnp.where(place <= time, jnp.log1p(-beta_all), 0.0)
    log_now = jnp.sum(jnp.sum(log_all, axis=1, keepdims=True), axis=0, keepdims=True)
    beta = (0.0001 + (0.02 - 0.0001) * when / 999.0)[:1, :1]
    keep = jnp.exp(log_now)
    root = lax.rsqrt(1.0 - beta)
    of_state = root - 1.0
    of_noise = jnp.sqrt(beta)
    of_pred = -beta * root * lax.rsqrt(1.0 - keep)
    half = TEMB // 2
    lane = iota((8, TEMB), 1)
    angle = when * jnp.exp(-math.log(10000.0) * (lane & (half - 1)).astype(F32) / half)
    embed = jnp.where(lane < half, jnp.cos(angle), jnp.sin(angle)).astype(BF16)
    loads[3].wait()
    embed = dot(embed, tw[...])[:1]
    time_scale, time_shift = 1.0 + embed[:, :CH], embed[:, CH:]

    loads[2].wait()
    head = jnp.where(step == 0, 1.0, 0.0)

    @pl.loop(0, 8)
    def _(r):
        here = st[:, pl.ds(pl.multiple_of(8 * r + 8, 8), 8), :].reshape(24, ROWS)
        push = no[:, pl.ds(pl.multiple_of(8 * r, 8), 8), :].reshape(24, ROWS)
        e_own[r] = (of_state + head) * here + of_noise * push

    pl.semaphore_wait(barrier, len(peers))
    halo = [
        send(st.at[:, pl.ds(64, 8), :], st.at[:, pl.ds(0, 8), :], halo_s.at[0], halo_r.at[0], at_quad(1)),
        send(st.at[:, pl.ds(8, 8), :], st.at[:, pl.ds(72, 8), :], halo_s.at[1], halo_r.at[1], at_quad(3)),
    ]


    def share_sums(k):
        return [
            send(stat_own.at[k], stat_in.at[k, j - 1], stat_s.at[3 * k + j - 1], stat_r.at[3 * k + j - 1], at_quad(j))
            for j in range(1, QUADS)
        ]

    def total_sums(k, copies):
        total = stat_own[k]
        for j, copy in enumerate(copies):
            copy.wait()
            total = total + stat_in[k, j]
        return scale_shift(total, float(QUADS * ROWS * CH // 32))

    stats = share_sums(0)

    def scatter(own_ref, in_ref, ss, rs):
        return [
            send(own_ref.at[spot_of(j)], in_ref.at[spot], ss.at[j], rs.at[j], at_spot(j))
            for j in FAR
        ]

    def to_lines(tot, line_in, ss, rs, start):
        for j in range(1, LINES):
            copy = pltpu.make_async_remote_copy(
                src_ref=tot, dst_ref=line_in.at[j], send_sem=ss.at[j], recv_sem=rs.at[j],
                device_id=at_line(j), device_id_type=MESH,
            )

            @pl.when(line + j < LINES)
            def _():
                if start:
                    copy.start()
                else:
                    copy.wait_send()

            if not start:

                @pl.when(line >= j)
                def _():
                    copy.wait_recv()

    def lines_sum(line_in, shape, load_one):
        base = jnp.zeros(shape, F32)
        for j in range(1, LINES):
            base = base + jnp.where(line >= j, load_one(line_in, j), 0.0)
        return base

    def back(pre, out_ref, ss, rs):
        return [
            send(pre.at[spot_of(j)], out_ref.at[spot], ss.at[j], rs.at[j], at_spot(j))
            for j in FAR
        ]

    early_a = scatter(e_own, e_in, ea_s, ea_r)

    for item in halo:
        item.wait()
    embed_row(0)
    embed_row(9)
    scale, shift = total_sums(0, stats)

    def activate(source, gain, bias):
        @pl.loop(0, 10)
        def _(r):
            where = pl.ds(pl.multiple_of(GRID * r, GRID), GRID)
            x = source[where, :] * gain + bias
            outside = ((quad == 0) & (r == 0)) | ((quad == QUADS - 1) & (r == 9))
            x = x * (jnp.tanh(0.5 * x) + 1.0) * jnp.where(outside, 0.0, 0.5)
            col = iota((GRID, CH), 0)
            act[0, where, :] = jnp.where(col == 0, 0.0, pltpu.roll(x, 1, axis=0)).astype(BF16)
            act[1, where, :] = x.astype(BF16)
            act[2, where, :] = jnp.where(col == GRID - 1, 0.0, pltpu.roll(x, GRID - 1, axis=0)).astype(BF16)

    def convolve(weight, n):
        total = None
        for row in range(3):
            for col in range(3):
                term = dot(
                    act[col, pl.ds(GRID * row, ROWS), :],
                    weight[pl.ds((3 * row + col) * CH, CH), pl.ds(256 * n, 256)],
                )
                total = term if total is None else total + term
        return total

    activate(hid, scale, shift)
    loads[4].wait()
    for n in range(2):
        inn[own, pl.ds(256 * n, 256)] = convolve(c1, n)
    stat_own[1] = sums_of(inn[own, :])
    stats = share_sums(1)
    middle = flat(stat_own[1]) / ROWS
    ihalo[0] = (inn[pl.ds(ROWS, EDGE), :] - middle).astype(BF16)
    ihalo[1] = (inn[pl.ds(EDGE, EDGE), :] - middle).astype(BF16)
    edges = [
        send(ihalo.at[0], ihalo.at[2], inn_s.at[0], inn_r.at[0], at_quad(1)),
        send(ihalo.at[1], ihalo.at[3], inn_s.at[1], inn_r.at[1], at_quad(3)),
    ]

    for item in early_a:
        item.wait()
    e_in[spot] = e_own[spot]
    run = jnp.zeros((24, ROWS), F32)
    for d in range(PLANE):
        e_pre[d] = run
        run = run + e_in[d]
    e_tot[...] = run
    to_lines(e_tot, e_line, eb_s, eb_r, True)
    loads[6].wait()
    wqt[...] = aw[:, :CH].T

    scale, shift = total_sums(1, stats)
    for item in edges:
        item.wait()
    inn[pl.ds(0, EDGE), :] = ihalo[2].astype(F32) + flat(stat_in[1, 0]) / ROWS
    inn[pl.ds(ALL - EDGE, EDGE), :] = ihalo[3].astype(F32) + flat(stat_in[1, 2]) / ROWS
    activate(inn, scale * time_scale, shift * time_scale + time_shift)
    loads[5].wait()
    for n in range(2):
        lanes = pl.ds(256 * n, 256)
        blk[:, lanes] = hid[own, lanes] + convolve(c2, n)
    stat_own[2] = sums_of(blk[...])
    stats = share_sums(2)
    raw[0] = (blk[...] - flat(stat_own[2]) / ROWS).astype(BF16)
    low, high = pl.ds(0, 128), pl.ds(128, 128)
    low_r = send(raw.at[0, low], raw.at[1, low], gat_s.at[0], gat_r.at[0], at_quad(1))
    high_l = send(raw.at[0, high], raw.at[2, high], gat_s.at[1], gat_r.at[1], at_quad(3))
    high_r = send(raw.at[0, high], raw.at[1, high], gat_s.at[2], gat_r.at[2], at_quad(1))
    low_l = send(raw.at[0, low], raw.at[2, low], gat_s.at[3], gat_r.at[3], at_quad(3))


    to_lines(e_tot, e_line, eb_s, eb_r, False)
    base = lines_sum(e_line, (24, ROWS), lambda ref, j: ref[j])
    for d in range(PLANE):
        e_pre[d] = e_pre[d] + base
    early_c = back(e_pre, e_out, ec_s, ec_r)
    wvt[...] = aw[:, 2 * CH :].T

    scale, shift = total_sums(2, stats)
    normed = (blk[...] * scale + shift).astype(BF16)
    queries = dot_nt(wqt[...], normed).astype(BF16)
    upper = iota((128, ROWS), 0) < 64
    for p in range(4):
        pair = queries[128 * p : 128 * (p + 1)]
        qz[2 * p] = jnp.where(upper, pair, jnp.zeros_like(pair))
        qz[2 * p + 1] = jnp.where(upper, jnp.zeros_like(pair), pair)
    sharp = math.log2(math.e) / 8.0

    def attend(slot, normed=None):
        if slot > 0:
            offset = flat(stat_in[2, (0, 2, 1)[slot - 1]]) / ROWS * scale + shift
            normed = (raw[slot].astype(F32) * scale + offset).astype(BF16)
        kbuf[...] = dot(normed, aw[:, CH : 2 * CH]).astype(BF16)
        vbuf[...] = dot_nt(wvt[...], normed).astype(BF16)

        def some(base):
            scores, most, weights, total = {}, {}, {}, {}
            for g in range(GROUP):
                h = base + g
                pair = pl.ds(pl.multiple_of(128 * (h // 2), 128), 128)
                scores[g] = dot(kbuf[:, pair], qz[h])
            for g in range(GROUP):
                h = base + g
                most[g] = jnp.max(scores[g], axis=0, keepdims=True)
                if slot > 0:
                    most[g] = jnp.maximum(most[g], mref[h])
                e = jnp.exp2((scores[g] - most[g]) * sharp)
                total[g] = jnp.sum(e, axis=0, keepdims=True)
                weights[g] = e.astype(BF16)
            for g in range(GROUP):
                h = base + g
                rows = pl.ds(pl.multiple_of(64 * h, 64), 64)
                value = dot(vbuf[rows, :], weights[g])
                if slot > 0:
                    fade = jnp.exp2((mref[h] - most[g]) * sharp)
                    total[g] = total[g] + lref[h] * fade
                    value = value + att[rows, :] * fade
                mref[h] = most[g]
                lref[h] = total[g]
                att[rows, :] = value

        if GROUP == HEADS:
            some(0)
        else:
            pl.loop(0, HEADS // GROUP)(lambda i: some(i * GROUP))

    attend(0, normed)
    low_r.wait_recv()
    pass_r = send(raw.at[1, low], raw.at[3, low], gat_s.at[4], gat_r.at[4], at_quad(1))
    high_l.wait_recv()
    pass_l = send(raw.at[2, high], raw.at[3, high], gat_s.at[5], gat_r.at[5], at_quad(3))
    loads[7].wait()
    loads[8].wait()
    prt[...] = pr[...].T
    blkt[...] = blk[...].T
    big[...] = (iota((ROWS, 8 * ROWS), 0) == iota((ROWS, 8 * ROWS), 1) >> 3).astype(F32).astype(BF16)
    for item in early_c:
        item.wait()
    e_out[spot] = e_pre[spot]
    for r in range(8):
        e_sum[:, pl.ds(8 * r, 8), :] = (e_out[r] + e_own[r]).reshape(3, 8, ROWS)
    early_copy = pltpu.make_async_copy(e_sum, early, early_sem.at[0])
    early_copy.start()
    high_r.wait_recv()
    attend(1)
    low_l.wait_recv()
    attend(2)
    pass_r.wait_recv()
    pass_l.wait_recv()
    attend(3)
    for h in range(HEADS):
        rows = pl.ds(64 * h, 64)
        att[rows, :] = att[rows, :] / lref[h]

    mixed = blkt[...] + dot(prt[...], att[...].astype(BF16))
    predicted = (dot(ow[...], mixed.astype(BF16)) * of_pred).astype(BF16)
    late_a = []
    for j in FAR + (0,):
        r = spot_of(j)
        wide = dot(predicted, big[:, pl.ds(pl.multiple_of(256 * r, 256), 256)])
        wide = jnp.where(diag, wide, 0.0).astype(BF16)
        p_own[r] = pack(lax.dot_general(spread, wide, (((0,), (0,)), ((), ())), preferred_element_type=F32))
        if j > 0:
            late_a.append(send(p_own.at[r], p_in.at[spot], pa_s.at[j], pa_r.at[j], at_spot(j)))

    p_in[spot] = p_own[spot]
    for item in late_a:
        item.wait()
    run = jnp.zeros((16, 384), F32)
    runs = []
    for d in range(PLANE):
        runs.append(run)
        run = run + p_in[d].astype(F32)
    p_tot[...] = run.astype(BF16)
    to_lines(p_tot, p_line, pb_s, pb_r, True)
    to_lines(p_tot, p_line, pb_s, pb_r, False)
    base = lines_sum(p_line, (16, 384), lambda ref, j: ref[j].astype(F32))
    for d in range(PLANE):
        p_pre[d] = runs[d] + base
    late_c = back(p_pre, p_out, pc_s, pc_r)
    p_out[spot] = p_pre[spot]
    for item in late_c:
        item.wait()
    for r in range(8):
        late[:, pl.ds(8 * r, 8), :] = (unpack(p_out[r]) + unpack(p_own[r])).reshape(3, 8, ROWS)
    early_copy.wait()
    for item in (low_r, high_l, high_r, low_l, pass_r, pass_l):
        item.wait_send()


def body(states, noise, ws, pw, tw, c1, c2, aw, pr, ow):
    dma = pltpu.SemaphoreType.DMA
    vmem = pltpu.VMEM
    anyhow = pl.BlockSpec(memory_space=pl.ANY)
    chunk, small = (24, ROWS), (16, 384)
    scratch = [
        vmem((3, 80, 256), F32), vmem((3, 64, 256), F32),
        vmem((FEAT, CH), BF16), vmem((TEMB, 2 * CH), BF16),
        vmem((9 * CH, CH), BF16), vmem((9 * CH, CH), BF16),
        vmem((CH, 3 * CH), BF16), vmem((CH, CH), BF16), vmem((FEAT, CH), BF16),
        vmem((CH, CH), BF16), vmem((CH, CH), BF16), vmem((CH, CH), BF16),
        vmem((ALL, CH), F32), vmem((3, ALL, CH), BF16), vmem((ALL, CH), F32),
        vmem((ROWS, CH), F32), vmem((CH, ROWS), F32),
        vmem((ROWS, CH), BF16), vmem((CH, ROWS), BF16),
        vmem((8, 128, ROWS), BF16), vmem((CH, ROWS), F32),
        vmem((8, 1, ROWS), F32), vmem((8, 1, ROWS), F32), vmem((ROWS, 8 * ROWS), BF16),
        vmem((3, 8, 128), F32), vmem((3, 3, 8, 128), F32),
        vmem((8,) + chunk, F32), vmem((8,) + chunk, F32), vmem(chunk, F32), vmem((8,) + chunk, F32),
        vmem((8,) + chunk, F32), vmem((8,) + chunk, F32),
        vmem((3, 64, 256), F32), vmem((4, EDGE, CH), BF16), vmem((4, ROWS, CH), BF16),
        vmem((8,) + small, BF16), vmem((8,) + small, BF16), vmem(small, BF16), vmem((8,) + small, BF16),
        vmem((8,) + small, F32), vmem((8,) + small, F32),
        dma((9,)), dma((1,)), dma((2,)), dma((2,)), dma((9,)), dma((9,)), dma((2,)), dma((2,)), dma((6,)), dma((6,)),
    ] + [dma((8,)) for _ in range(12)]
    early, late = pl.pallas_call(
        kernel,
        out_shape=[jax.ShapeDtypeStruct((3, 64, 256), F32)] * 2,
        in_specs=[anyhow, anyhow, pl.BlockSpec(memory_space=pltpu.SMEM)] + [anyhow] * 7,
        out_specs=[anyhow, pl.BlockSpec(memory_space=pltpu.VMEM)],
        scratch_shapes=scratch,
        compiler_params=pltpu.CompilerParams(
            collective_id=0, has_side_effects=True, vmem_limit_bytes=56 * 1024 * 1024
        ),
    )(
        states[0], noise[0], ws, pw, tw,
        c1.reshape(9 * CH, CH), c2.reshape(9 * CH, CH), aw, pr, ow.T,
    )
    return (early + late)[None]


def solution(mesh):
    image = P("step", None, "quad", None)
    return jax.shard_map(
        body,
        mesh=mesh,
        in_specs=(image, image) + (P(),) * 8,
        out_specs=image,
        check_vma=False,
    )
```

```python
import math

import jax
import jax.numpy as jnp
from jax import lax
from jax.experimental import pallas as pl
from jax.experimental.pallas import tpu as pltpu
from jax.sharding import PartitionSpec as P

CH = 512
HEADS = 8
GROUP = 8
FAR = (5, 4, 3, 7, 2, 6, 1)
PATCH = 8
TEMB = 128
FEAT = 192
GRID = 32
ROWS = 256
EDGE = 32
ALL = ROWS + 2 * EDGE
PLANE = 8
LINES = 8
QUADS = 4
EPS = 1e-05
MESH = pl.DeviceIdType.MESH
F32 = jnp.float32
BF16 = jnp.bfloat16
NT = (((1,), (1,)), ((), ()))


def iota(shape, dim):
    return lax.broadcasted_iota(jnp.int32, shape, dim)


def dot(a, b):
    return jnp.dot(a, b, preferred_element_type=F32)


def dot_nt(a, b):
    return lax.dot_general(a, b, NT, preferred_element_type=F32)


def pack(x):
    low = jnp.concatenate([x[16:24, :128], x[16:24, 128:]], axis=0)
    return jnp.concatenate([x[:16], low], axis=1).astype(BF16)


def unpack(y):
    y = y.astype(F32)
    low = jnp.concatenate([y[:8, 256:], y[8:, 256:]], axis=1)
    return jnp.concatenate([y[:, :256], low], axis=0)


def flat(v):
    return jnp.concatenate([v[i : i + 1] for i in range(4)], axis=1)


def sums_of(x):
    def fold(v):
        v = jnp.sum(v, axis=0, keepdims=True)
        return [v[:, 128 * i : 128 * (i + 1)] for i in range(4)]

    return jnp.concatenate(fold(x) + fold(x * x), axis=0)


def scale_shift(total, count):
    lane = iota((8, 128), 1)
    for s in (1, 2, 4, 8):
        up = pltpu.roll(total, 128 - s, axis=1)
        down = pltpu.roll(total, s, axis=1)
        total = total + jnp.where((lane & s) == 0, up, down)
    total = total / count
    mean, square = total[:4], total[4:]
    rstd = lax.rsqrt(square - mean * mean + EPS)
    shift = -mean * rstd
    return flat(rstd), flat(shift)


def kernel(
    st_h, no_h, ws, pw_h, tw_h, c1_h, c2_h, aw_h, pr_h, ow_h, early, late,
    st, no, pw, tw, c1, c2, aw, pr, ow, wqt, wvt, prt,
    hid, act, inn, blk, blkt, kbuf, vbuf, qz, att, mref, lref, big,
    stat_own, stat_in, e_own, e_in, e_tot, e_line, e_pre, e_out, e_sum, ihalo, raw,
    p_own, p_in, p_tot, p_line, p_pre, p_out,
    load, early_sem, halo_s, halo_r, stat_s, stat_r, inn_s, inn_r, gat_s, gat_r,
    ea_s, ea_r, eb_s, eb_r, ec_s, ec_r, pa_s, pa_r, pb_s, pb_r, pc_s, pc_r,
):
    step = lax.axis_index("step")
    quad = lax.axis_index("quad")
    line = step // PLANE
    spot = step % PLANE


    def at_quad(j):
        return (step, (quad + j) % QUADS)

    def spot_of(j):
        return ((spot // 2 + j // 2) % 4) * 2 + (spot + j) % 2

    def at_spot(j):
        return (line * PLANE + spot_of(j), quad)

    def at_line(j):
        return (((line + j) % LINES) * PLANE + spot, quad)

    barrier = pltpu.get_barrier_semaphore()
    peers = [at_line(j) for j in (4, 3, 5, 2, 6, 1, 7)]
    peers += [at_spot(j) for j in FAR]
    peers += [at_quad(j) for j in range(1, QUADS)]
    for peer in peers:
        pl.semaphore_signal(barrier, inc=1, device_id=peer, device_id_type=MESH)

    def send(src, dst, ss, rs, peer):
        copy = pltpu.make_async_remote_copy(
            src_ref=src, dst_ref=dst, send_sem=ss, recv_sem=rs, device_id=peer, device_id_type=MESH
        )
        copy.start()
        return copy

    loads = [
        pltpu.make_async_copy(st_h, st.at[:, pl.ds(8, 64), :], load.at[0]),
        pltpu.make_async_copy(pw_h, pw, load.at[1]),
        pltpu.make_async_copy(no_h, no, load.at[2]),
        pltpu.make_async_copy(tw_h, tw, load.at[3]),
        pltpu.make_async_copy(c1_h, c1, load.at[4]),
        pltpu.make_async_copy(c2_h, c2, load.at[5]),
        pltpu.make_async_copy(aw_h, aw, load.at[6]),
        pltpu.make_async_copy(pr_h, pr, load.at[7]),
        pltpu.make_async_copy(ow_h, ow, load.at[8]),
    ]
    for item in loads:
        item.start()
    feat = iota((FEAT, ROWS), 0)
    pixel = iota((FEAT, ROWS), 1)
    diag = (feat & 7) == (pixel & 7)
    spread = (iota((FEAT, 24), 0) >> 3 == iota((FEAT, 24), 1)).astype(F32).astype(BF16)
    big[...] = (iota((ROWS, 8 * ROWS), 0) == iota((ROWS, 8 * ROWS), 1) >> 3).astype(F32).astype(BF16)

    def on_diag(v):
        pieces = [v[:, i : i + ROWS] for i in range(0, v.shape[1], ROWS)]
        return jnp.concatenate([jnp.where(diag, piece, 0.0) for piece in pieces], axis=1).astype(BF16)


    loads[0].wait()
    loads[1].wait()

    inside = [st[:, pl.ds(8 * r, 8), :].reshape(24, ROWS) for r in range(1, 9)]
    wide = dot(spread, jnp.concatenate(inside, axis=1).astype(BF16))
    patches = dot_nt(big[...], on_diag(wide)).astype(BF16)
    hid[pl.ds(EDGE, ROWS), :] = dot(patches, pw[...])
    own = pl.ds(EDGE, ROWS)
    stat_own[0] = sums_of(hid[own, :])

    pl.semaphore_wait(barrier, len(peers))
    halo = [
        send(st.at[:, pl.ds(64, 8), :], st.at[:, pl.ds(0, 8), :], halo_s.at[0], halo_r.at[0], at_quad(1)),
        send(st.at[:, pl.ds(8, 8), :], st.at[:, pl.ds(72, 8), :], halo_s.at[1], halo_r.at[1], at_quad(3)),
    ]


    def share_sums(k):
        return [
            send(stat_own.at[k], stat_in.at[k, j - 1], stat_s.at[3 * k + j - 1], stat_r.at[3 * k + j - 1], at_quad(j))
            for j in range(1, QUADS)
        ]

    def total_sums(k, copies):
        total = stat_own[k]
        for j, copy in enumerate(copies):
            copy.wait()
            total = total + stat_in[k, j]
        return scale_shift(total, float(QUADS * ROWS * CH // 32))

    stats = share_sums(0)

    time = 999 - ws[0] - step
    when = jnp.full((8, 128), time.astype(F32))
    place = iota((8, 128), 0) * 128 + iota((8, 128), 1)
    beta_all = 0.0001 + (0.02 - 0.0001) * place.astype(F32) / 999.0
    log_all = jnp.where(place <= time, jnp.log1p(-beta_all), 0.0)
    log_now = jnp.sum(jnp.sum(log_all, axis=1, keepdims=True), axis=0, keepdims=True)
    beta = (0.0001 + (0.02 - 0.0001) * when / 999.0)[:1, :1]
    keep = jnp.exp(log_now)
    root = lax.rsqrt(1.0 - beta)
    of_state = root - 1.0
    of_noise = jnp.sqrt(beta)
    of_pred = -beta * root * lax.rsqrt(1.0 - keep)
    half = TEMB // 2
    lane = iota((8, TEMB), 1)
    angle = when * jnp.exp(-math.log(10000.0) * (lane & (half - 1)).astype(F32) / half)
    embed = jnp.where(lane < half, jnp.cos(angle), jnp.sin(angle)).astype(BF16)
    loads[3].wait()
    embed = dot(embed, tw[...])[:1]
    time_scale, time_shift = 1.0 + embed[:, :CH], embed[:, CH:]

    loads[2].wait()
    head = jnp.where(step == 0, 1.0, 0.0)

    @pl.loop(0, 8)
    def _(r):
        here = st[:, pl.ds(pl.multiple_of(8 * r + 8, 8), 8), :].reshape(24, ROWS)
        push = no[:, pl.ds(pl.multiple_of(8 * r, 8), 8), :].reshape(24, ROWS)
        e_own[r] = (of_state + head) * here + of_noise * push

    def scatter(own_ref, in_ref, ss, rs):
        return [
            send(own_ref.at[spot_of(j)], in_ref.at[spot], ss.at[j], rs.at[j], at_spot(j))
            for j in FAR
        ]

    def to_lines(tot, line_in, ss, rs, start):
        for j in range(1, LINES):
            copy = pltpu.make_async_remote_copy(
                src_ref=tot, dst_ref=line_in.at[j], send_sem=ss.at[j], recv_sem=rs.at[j],
                device_id=at_line(j), device_id_type=MESH,
            )

            @pl.when(line + j < LINES)
            def _():
                if start:
                    copy.start()
                else:
                    copy.wait_send()

            if not start:

                @pl.when(line >= j)
                def _():
                    copy.wait_recv()

    def lines_sum(line_in, shape, load_one):
        base = jnp.zeros(shape, F32)
        for j in range(1, LINES):
            base = base + jnp.where(line >= j, load_one(line_in, j), 0.0)
        return base

    def back(pre, out_ref, ss, rs):
        return [
            send(pre.at[spot_of(j)], out_ref.at[spot], ss.at[j], rs.at[j], at_spot(j))
            for j in FAR
        ]

    early_a = scatter(e_own, e_in, ea_s, ea_r)

    for item in halo:
        item.wait()
    outer = [st[:, pl.ds(8 * r, 8), :].reshape(24, ROWS) for r in (0, 9)]
    wide = on_diag(dot(spread, jnp.concatenate(outer, axis=1).astype(BF16)))
    patches = dot_nt(big[0 : 2 * GRID, 0 : 2 * ROWS], wide).astype(BF16)
    edge_rows = dot(patches, pw[...])
    hid[pl.ds(0, EDGE), :] = edge_rows[:EDGE]
    hid[pl.ds(ALL - EDGE, EDGE), :] = edge_rows[EDGE:]
    scale, shift = total_sums(0, stats)

    def activate(source, gain, bias):
        @pl.loop(0, 10)
        def _(r):
            where = pl.ds(pl.multiple_of(GRID * r, GRID), GRID)
            x = source[where, :] * gain + bias
            outside = ((quad == 0) & (r == 0)) | ((quad == QUADS - 1) & (r == 9))
            x = x * (jnp.tanh(0.5 * x) + 1.0) * jnp.where(outside, 0.0, 0.5)
            col = iota((GRID, CH), 0)
            act[0, where, :] = jnp.where(col == 0, 0.0, pltpu.roll(x, 1, axis=0)).astype(BF16)
            act[1, where, :] = x.astype(BF16)
            act[2, where, :] = jnp.where(col == GRID - 1, 0.0, pltpu.roll(x, GRID - 1, axis=0)).astype(BF16)

    def convolve(weight, n):
        total = None
        for row in range(3):
            for col in range(3):
                term = dot(
                    act[col, pl.ds(GRID * row, ROWS), :],
                    weight[pl.ds((3 * row + col) * CH, CH), pl.ds(256 * n, 256)],
                )
                total = term if total is None else total + term
        return total

    activate(hid, scale, shift)
    loads[4].wait()
    for n in range(2):
        inn[own, pl.ds(256 * n, 256)] = convolve(c1, n)
    stat_own[1] = sums_of(inn[own, :])
    stats = share_sums(1)
    middle = flat(stat_own[1]) / ROWS
    ihalo[0] = (inn[pl.ds(ROWS, EDGE), :] - middle).astype(BF16)
    ihalo[1] = (inn[pl.ds(EDGE, EDGE), :] - middle).astype(BF16)
    edges = [
        send(ihalo.at[0], ihalo.at[2], inn_s.at[0], inn_r.at[0], at_quad(1)),
        send(ihalo.at[1], ihalo.at[3], inn_s.at[1], inn_r.at[1], at_quad(3)),
    ]

    for item in early_a:
        item.wait()
    e_in[spot] = e_own[spot]
    run = jnp.zeros((24, ROWS), F32)
    for d in range(PLANE):
        e_pre[d] = run
        run = run + e_in[d]
    e_tot[...] = run
    to_lines(e_tot, e_line, eb_s, eb_r, True)
    loads[6].wait()
    wqt[...] = aw[:, :CH].T

    scale, shift = total_sums(1, stats)
    for item in edges:
        item.wait()
    inn[pl.ds(0, EDGE), :] = ihalo[2].astype(F32) + flat(stat_in[1, 0]) / ROWS
    inn[pl.ds(ALL - EDGE, EDGE), :] = ihalo[3].astype(F32) + flat(stat_in[1, 2]) / ROWS
    activate(inn, scale * time_scale, shift * time_scale + time_shift)
    loads[5].wait()
    for n in range(2):
        lanes = pl.ds(256 * n, 256)
        blk[:, lanes] = hid[own, lanes] + convolve(c2, n)
    stat_own[2] = sums_of(blk[...])
    stats = share_sums(2)
    raw[0] = (blk[...] - flat(stat_own[2]) / ROWS).astype(BF16)
    low, high = pl.ds(0, 128), pl.ds(128, 128)
    low_r = send(raw.at[0, low], raw.at[1, low], gat_s.at[0], gat_r.at[0], at_quad(1))
    high_l = send(raw.at[0, high], raw.at[2, high], gat_s.at[1], gat_r.at[1], at_quad(3))
    high_r = send(raw.at[0, high], raw.at[1, high], gat_s.at[2], gat_r.at[2], at_quad(1))
    low_l = send(raw.at[0, low], raw.at[2, low], gat_s.at[3], gat_r.at[3], at_quad(3))


    to_lines(e_tot, e_line, eb_s, eb_r, False)
    base = lines_sum(e_line, (24, ROWS), lambda ref, j: ref[j])
    for d in range(PLANE):
        e_pre[d] = e_pre[d] + base
    early_c = back(e_pre, e_out, ec_s, ec_r)
    wvt[...] = aw[:, 2 * CH :].T

    scale, shift = total_sums(2, stats)
    normed = (blk[...] * scale + shift).astype(BF16)
    queries = dot_nt(wqt[...], normed).astype(BF16)
    upper = iota((128, ROWS), 0) < 64
    for p in range(4):
        pair = queries[128 * p : 128 * (p + 1)]
        qz[2 * p] = jnp.where(upper, pair, jnp.zeros_like(pair))
        qz[2 * p + 1] = jnp.where(upper, jnp.zeros_like(pair), pair)
    sharp = math.log2(math.e) / 8.0

    def attend(slot, normed=None):
        if slot > 0:
            offset = flat(stat_in[2, (0, 2, 1)[slot - 1]]) / ROWS * scale + shift
            normed = (raw[slot].astype(F32) * scale + offset).astype(BF16)
        kbuf[...] = dot(normed, aw[:, CH : 2 * CH]).astype(BF16)
        vbuf[...] = dot_nt(wvt[...], normed).astype(BF16)

        def some(base):
            scores, most, weights, total = {}, {}, {}, {}
            for g in range(GROUP):
                h = base + g
                pair = pl.ds(pl.multiple_of(128 * (h // 2), 128), 128)
                scores[g] = dot(kbuf[:, pair], qz[h])
            for g in range(GROUP):
                h = base + g
                most[g] = jnp.max(scores[g], axis=0, keepdims=True)
                if slot > 0:
                    most[g] = jnp.maximum(most[g], mref[h])
                e = jnp.exp2((scores[g] - most[g]) * sharp)
                total[g] = jnp.sum(e, axis=0, keepdims=True)
                weights[g] = e.astype(BF16)
            for g in range(GROUP):
                h = base + g
                rows = pl.ds(pl.multiple_of(64 * h, 64), 64)
                value = dot(vbuf[rows, :], weights[g])
                if slot > 0:
                    fade = jnp.exp2((mref[h] - most[g]) * sharp)
                    total[g] = total[g] + lref[h] * fade
                    value = value + att[rows, :] * fade
                mref[h] = most[g]
                lref[h] = total[g]
                att[rows, :] = value

        if GROUP == HEADS:
            some(0)
        else:
            pl.loop(0, HEADS // GROUP)(lambda i: some(i * GROUP))

    attend(0, normed)
    low_r.wait_recv()
    pass_r = send(raw.at[1, low], raw.at[3, low], gat_s.at[4], gat_r.at[4], at_quad(1))
    high_l.wait_recv()
    pass_l = send(raw.at[2, high], raw.at[3, high], gat_s.at[5], gat_r.at[5], at_quad(3))
    loads[7].wait()
    loads[8].wait()
    prt[...] = pr[...].T
    blkt[...] = blk[...].T
    for item in early_c:
        item.wait()
    e_out[spot] = e_pre[spot]
    for r in range(8):
        e_sum[:, pl.ds(8 * r, 8), :] = (e_out[r] + e_own[r]).reshape(3, 8, ROWS)
    early_copy = pltpu.make_async_copy(e_sum, early, early_sem.at[0])
    early_copy.start()
    high_r.wait_recv()
    attend(1)
    low_l.wait_recv()
    attend(2)
    pass_r.wait_recv()
    pass_l.wait_recv()
    attend(3)
    for h in range(HEADS):
        rows = pl.ds(64 * h, 64)
        att[rows, :] = att[rows, :] / lref[h]

    mixed = blkt[...] + dot(prt[...], att[...].astype(BF16))
    predicted = (dot(ow[...], mixed.astype(BF16)) * of_pred).astype(BF16)
    wide = dot(predicted, big[...])
    wide = lax.dot_general(spread, on_diag(wide), (((0,), (0,)), ((), ())), preferred_element_type=F32)
    for r in range(8):
        p_own[r] = pack(wide[:, 256 * r : 256 * (r + 1)])
    late_a = scatter(p_own, p_in, pa_s, pa_r)
    p_in[spot] = p_own[spot]
    for item in late_a:
        item.wait()
    run = jnp.zeros((16, 384), F32)
    runs = []
    for d in range(PLANE):
        runs.append(run)
        run = run + p_in[d].astype(F32)
    p_tot[...] = run.astype(BF16)
    to_lines(p_tot, p_line, pb_s, pb_r, True)
    to_lines(p_tot, p_line, pb_s, pb_r, False)
    base = lines_sum(p_line, (16, 384), lambda ref, j: ref[j].astype(F32))
    for d in range(PLANE):
        p_pre[d] = runs[d] + base
    late_c = back(p_pre, p_out, pc_s, pc_r)
    p_out[spot] = p_pre[spot]
    for item in late_c:
        item.wait()
    for r in range(8):
        late[:, pl.ds(8 * r, 8), :] = (unpack(p_out[r]) + unpack(p_own[r])).reshape(3, 8, ROWS)
    early_copy.wait()
    for item in (low_r, high_l, high_r, low_l, pass_r, pass_l):
        item.wait_send()


def body(states, noise, ws, pw, tw, c1, c2, aw, pr, ow):
    dma = pltpu.SemaphoreType.DMA
    vmem = pltpu.VMEM
    anyhow = pl.BlockSpec(memory_space=pl.ANY)
    chunk, small = (24, ROWS), (16, 384)
    scratch = [
        vmem((3, 80, 256), F32), vmem((3, 64, 256), F32),
        vmem((FEAT, CH), BF16), vmem((TEMB, 2 * CH), BF16),
        vmem((9 * CH, CH), BF16), vmem((9 * CH, CH), BF16),
        vmem((CH, 3 * CH), BF16), vmem((CH, CH), BF16), vmem((FEAT, CH), BF16),
        vmem((CH, CH), BF16), vmem((CH, CH), BF16), vmem((CH, CH), BF16),
        vmem((ALL, CH), F32), vmem((3, ALL, CH), BF16), vmem((ALL, CH), F32),
        vmem((ROWS, CH), F32), vmem((CH, ROWS), F32),
        vmem((ROWS, CH), BF16), vmem((CH, ROWS), BF16),
        vmem((8, 128, ROWS), BF16), vmem((CH, ROWS), F32),
        vmem((8, 1, ROWS), F32), vmem((8, 1, ROWS), F32), vmem((ROWS, 8 * ROWS), BF16),
        vmem((3, 8, 128), F32), vmem((3, 3, 8, 128), F32),
        vmem((8,) + chunk, F32), vmem((8,) + chunk, F32), vmem(chunk, F32), vmem((8,) + chunk, F32),
        vmem((8,) + chunk, F32), vmem((8,) + chunk, F32),
        vmem((3, 64, 256), F32), vmem((4, EDGE, CH), BF16), vmem((4, ROWS, CH), BF16),
        vmem((8,) + small, BF16), vmem((8,) + small, BF16), vmem(small, BF16), vmem((8,) + small, BF16),
        vmem((8,) + small, F32), vmem((8,) + small, F32),
        dma((9,)), dma((1,)), dma((2,)), dma((2,)), dma((9,)), dma((9,)), dma((2,)), dma((2,)), dma((6,)), dma((6,)),
    ] + [dma((8,)) for _ in range(12)]
    early, late = pl.pallas_call(
        kernel,
        out_shape=[jax.ShapeDtypeStruct((3, 64, 256), F32)] * 2,
        in_specs=[anyhow, anyhow, pl.BlockSpec(memory_space=pltpu.SMEM)] + [anyhow] * 7,
        out_specs=[anyhow, pl.BlockSpec(memory_space=pltpu.VMEM)],
        scratch_shapes=scratch,
        compiler_params=pltpu.CompilerParams(
            collective_id=0, has_side_effects=True, vmem_limit_bytes=56 * 1024 * 1024
        ),
    )(
        states[0], noise[0], ws, pw, tw,
        c1.reshape(9 * CH, CH), c2.reshape(9 * CH, CH), aw, pr, ow.T,
    )
    return (early + late)[None]


def solution(mesh):
    image = P("step", None, "quad", None)
    return jax.shard_map(
        body,
        mesh=mesh,
        in_specs=(image, image) + (P(),) * 8,
        out_specs=image,
        check_vma=False,
    )
```

```python
import math

import jax
import jax.numpy as jnp
from jax import lax
from jax.experimental import pallas as pl
from jax.experimental.pallas import tpu as pltpu
from jax.sharding import PartitionSpec as P

CH = 512
HEADS = 8
GROUP = 8
FAR = (5, 4, 3, 7, 2, 6, 1)
PATCH = 8
TEMB = 128
FEAT = 192
GRID = 32
ROWS = 256
EDGE = 32
ALL = ROWS + 2 * EDGE
PLANE = 8
LINES = 8
QUADS = 4
EPS = 1e-05
MESH = pl.DeviceIdType.MESH
F32 = jnp.float32
BF16 = jnp.bfloat16
NT = (((1,), (1,)), ((), ()))


def iota(shape, dim):
    return lax.broadcasted_iota(jnp.int32, shape, dim)


def dot(a, b):
    return jnp.dot(a, b, preferred_element_type=F32)


def dot_nt(a, b):
    return lax.dot_general(a, b, NT, preferred_element_type=F32)


def pack(x):
    low = jnp.concatenate([x[16:24, :128], x[16:24, 128:]], axis=0)
    return jnp.concatenate([x[:16], low], axis=1).astype(BF16)


def unpack(y):
    y = y.astype(F32)
    low = jnp.concatenate([y[:8, 256:], y[8:, 256:]], axis=1)
    return jnp.concatenate([y[:, :256], low], axis=0)


def flat(v):
    return jnp.concatenate([v[i : i + 1] for i in range(4)], axis=1)


def sums_of(x):
    def fold(v):
        v = jnp.sum(v, axis=0, keepdims=True)
        return [v[:, 128 * i : 128 * (i + 1)] for i in range(4)]

    return jnp.concatenate(fold(x) + fold(x * x), axis=0)


def scale_shift(total, count):
    lane = iota((8, 128), 1)
    for s in (1, 2, 4, 8):
        up = pltpu.roll(total, 128 - s, axis=1)
        down = pltpu.roll(total, s, axis=1)
        total = total + jnp.where((lane & s) == 0, up, down)
    total = total / count
    mean, square = total[:4], total[4:]
    rstd = lax.rsqrt(square - mean * mean + EPS)
    shift = -mean * rstd
    return flat(rstd), flat(shift)


def kernel(
    st_h, no_h, ws, pw_h, tw_h, c1_h, c2_h, aw_h, pr_h, ow_h, early, late,
    st, no, pw, tw, c1, c2, aw, pr, ow, wqt, wvt, prt,
    hid, act, inn, blk, blkt, kbuf, vbuf, qz, att, mref, lref, big,
    stat_own, stat_in, e_own, e_in, e_tot, e_line, e_pre, e_out, e_sum, ihalo, raw,
    p_own, p_in, p_tot, p_line, p_pre, p_out,
    load, early_sem, halo_s, halo_r, stat_s, stat_r, inn_s, inn_r, gat_s, gat_r,
    ea_s, ea_r, eb_s, eb_r, ec_s, ec_r, pa_s, pa_r, pb_s, pb_r, pc_s, pc_r,
):
    step = lax.axis_index("step")
    quad = lax.axis_index("quad")
    line = step // PLANE
    spot = step % PLANE


    def at_quad(j):
        return (step, (quad + j) % QUADS)

    def spot_of(j):
        return ((spot // 2 + j // 2) % 4) * 2 + (spot + j) % 2

    def at_spot(j):
        return (line * PLANE + spot_of(j), quad)

    def at_line(j):
        return (((line + j) % LINES) * PLANE + spot, quad)

    barrier = pltpu.get_barrier_semaphore()
    peers = [at_line(j) for j in (4, 3, 5, 2, 6, 1, 7)]
    peers += [at_spot(j) for j in FAR]
    peers += [at_quad(j) for j in range(1, QUADS)]
    for peer in peers:
        pl.semaphore_signal(barrier, inc=1, device_id=peer, device_id_type=MESH)

    def send(src, dst, ss, rs, peer):
        copy = pltpu.make_async_remote_copy(
            src_ref=src, dst_ref=dst, send_sem=ss, recv_sem=rs, device_id=peer, device_id_type=MESH
        )
        copy.start()
        return copy

    loads = [
        pltpu.make_async_copy(st_h, st.at[:, pl.ds(8, 64), :], load.at[0]),
        pltpu.make_async_copy(pw_h, pw, load.at[1]),
        pltpu.make_async_copy(no_h, no, load.at[2]),
        pltpu.make_async_copy(tw_h, tw, load.at[3]),
        pltpu.make_async_copy(c1_h, c1, load.at[4]),
        pltpu.make_async_copy(c2_h, c2, load.at[5]),
        pltpu.make_async_copy(aw_h, aw, load.at[6]),
        pltpu.make_async_copy(pr_h, pr, load.at[7]),
        pltpu.make_async_copy(ow_h, ow, load.at[8]),
    ]
    for item in loads:
        item.start()
    feat = iota((FEAT, ROWS), 0)
    pixel = iota((FEAT, ROWS), 1)
    diag = (feat & 7) == (pixel & 7)
    spread = (iota((FEAT, 24), 0) >> 3 == iota((FEAT, 24), 1)).astype(F32).astype(BF16)
    big[...] = (iota((ROWS, 8 * ROWS), 0) == iota((ROWS, 8 * ROWS), 1) >> 3).astype(F32).astype(BF16)

    def on_diag(v):
        pieces = [v[:, i : i + ROWS] for i in range(0, v.shape[1], ROWS)]
        return jnp.concatenate([jnp.where(diag, piece, 0.0) for piece in pieces], axis=1).astype(BF16)


    loads[0].wait()
    loads[1].wait()

    inside = [st[:, pl.ds(8 * r, 8), :].reshape(24, ROWS) for r in range(1, 9)]
    wide = dot(spread, jnp.concatenate(inside, axis=1).astype(BF16))
    patches = dot_nt(big[...], on_diag(wide)).astype(BF16)
    hid[pl.ds(EDGE, ROWS), :] = dot(patches, pw[...])
    own = pl.ds(EDGE, ROWS)
    stat_own[0] = sums_of(hid[own, :])

    pl.semaphore_wait(barrier, len(peers))
    halo = [
        send(st.at[:, pl.ds(64, 8), :], st.at[:, pl.ds(0, 8), :], halo_s.at[0], halo_r.at[0], at_quad(1)),
        send(st.at[:, pl.ds(8, 8), :], st.at[:, pl.ds(72, 8), :], halo_s.at[1], halo_r.at[1], at_quad(3)),
    ]


    def share_sums(k):
        return [
            send(stat_own.at[k], stat_in.at[k, j - 1], stat_s.at[3 * k + j - 1], stat_r.at[3 * k + j - 1], at_quad(j))
            for j in range(1, QUADS)
        ]

    def total_sums(k, copies):
        total = stat_own[k]
        for j, copy in enumerate(copies):
            copy.wait()
            total = total + stat_in[k, j]
        return scale_shift(total, float(QUADS * ROWS * CH // 32))

    stats = share_sums(0)

    time = 999 - ws[0] - step
    when = jnp.full((8, 128), time.astype(F32))
    place = iota((8, 128), 0) * 128 + iota((8, 128), 1)
    beta_all = 0.0001 + (0.02 - 0.0001) * place.astype(F32) / 999.0
    log_all = jnp.where(place <= time, jnp.log1p(-beta_all), 0.0)
    log_now = jnp.sum(jnp.sum(log_all, axis=1, keepdims=True), axis=0, keepdims=True)
    beta = (0.0001 + (0.02 - 0.0001) * when / 999.0)[:1, :1]
    keep = jnp.exp(log_now)
    root = lax.rsqrt(1.0 - beta)
    of_state = root - 1.0
    of_noise = jnp.sqrt(beta)
    of_pred = -beta * root * lax.rsqrt(1.0 - keep)
    half = TEMB // 2
    lane = iota((8, TEMB), 1)
    angle = when * jnp.exp(-math.log(10000.0) * (lane & (half - 1)).astype(F32) / half)
    embed = jnp.where(lane < half, jnp.cos(angle), jnp.sin(angle)).astype(BF16)
    loads[3].wait()
    embed = dot(embed, tw[...])[:1]
    time_scale, time_shift = 1.0 + embed[:, :CH], embed[:, CH:]

    loads[2].wait()
    head = jnp.where(step == 0, 1.0, 0.0)

    @pl.loop(0, 8)
    def _(r):
        here = st[:, pl.ds(pl.multiple_of(8 * r + 8, 8), 8), :].reshape(24, ROWS)
        push = no[:, pl.ds(pl.multiple_of(8 * r, 8), 8), :].reshape(24, ROWS)
        e_own[r] = (of_state + head) * here + of_noise * push

    def scatter(own_ref, in_ref, ss, rs):
        return [
            send(own_ref.at[spot_of(j)], in_ref.at[spot], ss.at[j], rs.at[j], at_spot(j))
            for j in FAR
        ]

    def to_lines(tot, line_in, ss, rs, start):
        for j in range(1, LINES):
            copy = pltpu.make_async_remote_copy(
                src_ref=tot, dst_ref=line_in.at[j], send_sem=ss.at[j], recv_sem=rs.at[j],
                device_id=at_line(j), device_id_type=MESH,
            )

            @pl.when(line + j < LINES)
            def _():
                if start:
                    copy.start()
                else:
                    copy.wait_send()

            if not start:

                @pl.when(line >= j)
                def _():
                    copy.wait_recv()

    def lines_sum(line_in, shape, load_one):
        base = jnp.zeros(shape, F32)
        for j in range(1, LINES):
            base = base + jnp.where(line >= j, load_one(line_in, j), 0.0)
        return base

    def back(pre, out_ref, ss, rs):
        return [
            send(pre.at[spot_of(j)], out_ref.at[spot], ss.at[j], rs.at[j], at_spot(j))
            for j in FAR
        ]

    early_a = scatter(e_own, e_in, ea_s, ea_r)

    for item in halo:
        item.wait()
    outer = [st[:, pl.ds(8 * r, 8), :].reshape(24, ROWS) for r in (0, 9)]
    wide = on_diag(dot(spread, jnp.concatenate(outer, axis=1).astype(BF16)))
    patches = dot_nt(big[0 : 2 * GRID, 0 : 2 * ROWS], wide).astype(BF16)
    edge_rows = dot(patches, pw[...])
    hid[pl.ds(0, EDGE), :] = edge_rows[:EDGE]
    hid[pl.ds(ALL - EDGE, EDGE), :] = edge_rows[EDGE:]
    scale, shift = total_sums(0, stats)

    def activate(source, gain, bias):
        @pl.loop(0, 10)
        def _(r):
            where = pl.ds(pl.multiple_of(GRID * r, GRID), GRID)
            x = source[where, :] * gain + bias
            outside = ((quad == 0) & (r == 0)) | ((quad == QUADS - 1) & (r == 9))
            x = x * (jnp.tanh(0.5 * x) + 1.0) * jnp.where(outside, 0.0, 0.5)
            col = iota((GRID, CH), 0)
            act[0, where, :] = jnp.where(col == 0, 0.0, pltpu.roll(x, 1, axis=0)).astype(BF16)
            act[1, where, :] = x.astype(BF16)
            act[2, where, :] = jnp.where(col == GRID - 1, 0.0, pltpu.roll(x, GRID - 1, axis=0)).astype(BF16)

    def convolve(weight, n):
        total = None
        for row in range(3):
            for col in range(3):
                term = dot(
                    act[col, pl.ds(GRID * row, ROWS), :],
                    weight[pl.ds((3 * row + col) * CH, CH), pl.ds(256 * n, 256)],
                )
                total = term if total is None else total + term
        return total

    activate(hid, scale, shift)
    loads[4].wait()
    for n in range(2):
        inn[own, pl.ds(256 * n, 256)] = convolve(c1, n)
    stat_own[1] = sums_of(inn[own, :])
    stats = share_sums(1)
    middle = flat(stat_own[1]) / ROWS
    ihalo[0] = (inn[pl.ds(ROWS, EDGE), :] - middle).astype(BF16)
    ihalo[1] = (inn[pl.ds(EDGE, EDGE), :] - middle).astype(BF16)
    edges = [
        send(ihalo.at[0], ihalo.at[2], inn_s.at[0], inn_r.at[0], at_quad(1)),
        send(ihalo.at[1], ihalo.at[3], inn_s.at[1], inn_r.at[1], at_quad(3)),
    ]

    for item in early_a:
        item.wait()
    e_in[spot] = e_own[spot]
    run = jnp.zeros((24, ROWS), F32)
    for d in range(PLANE):
        e_pre[d] = run
        run = run + e_in[d]
    e_tot[...] = run
    to_lines(e_tot, e_line, eb_s, eb_r, True)
    loads[6].wait()
    wqt[...] = aw[:, :CH].T

    scale, shift = total_sums(1, stats)
    for item in edges:
        item.wait()
    inn[pl.ds(0, EDGE), :] = ihalo[2].astype(F32) + flat(stat_in[1, 0]) / ROWS
    inn[pl.ds(ALL - EDGE, EDGE), :] = ihalo[3].astype(F32) + flat(stat_in[1, 2]) / ROWS
    activate(inn, scale * time_scale, shift * time_scale + time_shift)
    loads[5].wait()
    for n in range(2):
        lanes = pl.ds(256 * n, 256)
        blk[:, lanes] = hid[own, lanes] + convolve(c2, n)
    stat_own[2] = sums_of(blk[...])
    stats = share_sums(2)
    raw[0] = (blk[...] - flat(stat_own[2]) / ROWS).astype(BF16)
    low, high = pl.ds(0, 128), pl.ds(128, 128)
    low_r = send(raw.at[0, low], raw.at[1, low], gat_s.at[0], gat_r.at[0], at_quad(1))
    high_l = send(raw.at[0, high], raw.at[2, high], gat_s.at[1], gat_r.at[1], at_quad(3))
    high_r = send(raw.at[0, high], raw.at[1, high], gat_s.at[2], gat_r.at[2], at_quad(1))
    low_l = send(raw.at[0, low], raw.at[2, low], gat_s.at[3], gat_r.at[3], at_quad(3))


    to_lines(e_tot, e_line, eb_s, eb_r, False)
    base = lines_sum(e_line, (24, ROWS), lambda ref, j: ref[j])
    for d in range(PLANE):
        e_pre[d] = e_pre[d] + base
    early_c = back(e_pre, e_out, ec_s, ec_r)
    wvt[...] = aw[:, 2 * CH :].T

    scale, shift = total_sums(2, stats)
    normed = (blk[...] * scale + shift).astype(BF16)
    queries = dot_nt(wqt[...], normed).astype(BF16)
    upper = iota((128, ROWS), 0) < 64
    for p in range(4):
        pair = queries[128 * p : 128 * (p + 1)]
        qz[2 * p] = jnp.where(upper, pair, jnp.zeros_like(pair))
        qz[2 * p + 1] = jnp.where(upper, jnp.zeros_like(pair), pair)
    sharp = math.log2(math.e) / 8.0

    def attend(slots, normed=None):
        first, keys = slots == (0,), len(slots) * ROWS
        for i, slot in enumerate(slots):
            if slot > 0:
                offset = flat(stat_in[2, (0, 2, 1)[slot - 1]]) / ROWS * scale + shift
                normed = (raw[slot].astype(F32) * scale + offset).astype(BF16)
            kbuf[pl.ds(ROWS * i, ROWS), :] = dot(normed, aw[:, CH : 2 * CH]).astype(BF16)
            vbuf[:, pl.ds(ROWS * i, ROWS)] = dot_nt(wvt[...], normed).astype(BF16)

        def some(base):
            scores, most, weights, total = {}, {}, {}, {}
            for g in range(GROUP):
                h = base + g
                pair = pl.ds(pl.multiple_of(128 * (h // 2), 128), 128)
                scores[g] = dot(kbuf[0:keys, pair], qz[h])
            for g in range(GROUP):
                h = base + g
                most[g] = jnp.max(scores[g], axis=0, keepdims=True)
                if not first:
                    most[g] = jnp.maximum(most[g], mref[h])
                e = jnp.exp2((scores[g] - most[g]) * sharp)
                total[g] = jnp.sum(e, axis=0, keepdims=True)
                weights[g] = e.astype(BF16)
            for g in range(GROUP):
                h = base + g
                rows = pl.ds(pl.multiple_of(64 * h, 64), 64)
                value = dot(vbuf[rows, 0:keys], weights[g])
                if not first:
                    fade = jnp.exp2((mref[h] - most[g]) * sharp)
                    total[g] = total[g] + lref[h] * fade
                    value = value + att[rows, :] * fade
                mref[h] = most[g]
                lref[h] = total[g]
                att[rows, :] = value

        if GROUP == HEADS:
            some(0)
        else:
            pl.loop(0, HEADS // GROUP)(lambda i: some(i * GROUP))

    attend((0,), normed)
    low_r.wait_recv()
    pass_r = send(raw.at[1, low], raw.at[3, low], gat_s.at[4], gat_r.at[4], at_quad(1))
    high_l.wait_recv()
    pass_l = send(raw.at[2, high], raw.at[3, high], gat_s.at[5], gat_r.at[5], at_quad(3))
    loads[7].wait()
    loads[8].wait()
    prt[...] = pr[...].T
    blkt[...] = blk[...].T
    for item in early_c:
        item.wait()
    e_out[spot] = e_pre[spot]
    for r in range(8):
        e_sum[:, pl.ds(8 * r, 8), :] = (e_out[r] + e_own[r]).reshape(3, 8, ROWS)
    early_copy = pltpu.make_async_copy(e_sum, early, early_sem.at[0])
    early_copy.start()
    high_r.wait_recv()
    low_l.wait_recv()
    attend((1, 2))
    pass_r.wait_recv()
    pass_l.wait_recv()
    attend((3,))
    for h in range(HEADS):
        rows = pl.ds(64 * h, 64)
        att[rows, :] = att[rows, :] / lref[h]

    mixed = blkt[...] + dot(prt[...], att[...].astype(BF16))
    predicted = (dot(ow[...], mixed.astype(BF16)) * of_pred).astype(BF16)
    wide = dot(predicted, big[...])
    wide = lax.dot_general(spread, on_diag(wide), (((0,), (0,)), ((), ())), preferred_element_type=F32)
    for r in range(8):
        p_own[r] = pack(wide[:, 256 * r : 256 * (r + 1)])
    late_a = scatter(p_own, p_in, pa_s, pa_r)
    p_in[spot] = p_own[spot]
    for item in late_a:
        item.wait()
    run = jnp.zeros((16, 384), F32)
    runs = []
    for d in range(PLANE):
        runs.append(run)
        run = run + p_in[d].astype(F32)
    p_tot[...] = run.astype(BF16)
    to_lines(p_tot, p_line, pb_s, pb_r, True)
    to_lines(p_tot, p_line, pb_s, pb_r, False)
    base = lines_sum(p_line, (16, 384), lambda ref, j: ref[j].astype(F32))
    for d in range(PLANE):
        p_pre[d] = runs[d] + base
    late_c = back(p_pre, p_out, pc_s, pc_r)
    p_out[spot] = p_pre[spot]
    for item in late_c:
        item.wait()
    for r in range(8):
        late[:, pl.ds(8 * r, 8), :] = (unpack(p_out[r]) + unpack(p_own[r])).reshape(3, 8, ROWS)
    early_copy.wait()
    for item in (low_r, high_l, high_r, low_l, pass_r, pass_l):
        item.wait_send()


def body(states, noise, ws, pw, tw, c1, c2, aw, pr, ow):
    dma = pltpu.SemaphoreType.DMA
    vmem = pltpu.VMEM
    anyhow = pl.BlockSpec(memory_space=pl.ANY)
    chunk, small = (24, ROWS), (16, 384)
    scratch = [
        vmem((3, 80, 256), F32), vmem((3, 64, 256), F32),
        vmem((FEAT, CH), BF16), vmem((TEMB, 2 * CH), BF16),
        vmem((9 * CH, CH), BF16), vmem((9 * CH, CH), BF16),
        vmem((CH, 3 * CH), BF16), vmem((CH, CH), BF16), vmem((FEAT, CH), BF16),
        vmem((CH, CH), BF16), vmem((CH, CH), BF16), vmem((CH, CH), BF16),
        vmem((ALL, CH), F32), vmem((3, ALL, CH), BF16), vmem((ALL, CH), F32),
        vmem((ROWS, CH), F32), vmem((CH, ROWS), F32),
        vmem((2 * ROWS, CH), BF16), vmem((CH, 2 * ROWS), BF16),
        vmem((8, 128, ROWS), BF16), vmem((CH, ROWS), F32),
        vmem((8, 1, ROWS), F32), vmem((8, 1, ROWS), F32), vmem((ROWS, 8 * ROWS), BF16),
        vmem((3, 8, 128), F32), vmem((3, 3, 8, 128), F32),
        vmem((8,) + chunk, F32), vmem((8,) + chunk, F32), vmem(chunk, F32), vmem((8,) + chunk, F32),
        vmem((8,) + chunk, F32), vmem((8,) + chunk, F32),
        vmem((3, 64, 256), F32), vmem((4, EDGE, CH), BF16), vmem((4, ROWS, CH), BF16),
        vmem((8,) + small, BF16), vmem((8,) + small, BF16), vmem(small, BF16), vmem((8,) + small, BF16),
        vmem((8,) + small, F32), vmem((8,) + small, F32),
        dma((9,)), dma((1,)), dma((2,)), dma((2,)), dma((9,)), dma((9,)), dma((2,)), dma((2,)), dma((6,)), dma((6,)),
    ] + [dma((8,)) for _ in range(12)]
    early, late = pl.pallas_call(
        kernel,
        out_shape=[jax.ShapeDtypeStruct((3, 64, 256), F32)] * 2,
        in_specs=[anyhow, anyhow, pl.BlockSpec(memory_space=pltpu.SMEM)] + [anyhow] * 7,
        out_specs=[anyhow, pl.BlockSpec(memory_space=pltpu.VMEM)],
        scratch_shapes=scratch,
        compiler_params=pltpu.CompilerParams(
            collective_id=0, has_side_effects=True, vmem_limit_bytes=56 * 1024 * 1024
        ),
    )(
        states[0], noise[0], ws, pw, tw,
        c1.reshape(9 * CH, CH), c2.reshape(9 * CH, CH), aw, pr, ow.T,
    )
    return (early + late)[None]


def solution(mesh):
    image = P("step", None, "quad", None)
    return jax.shard_map(
        body,
        mesh=mesh,
        in_specs=(image, image) + (P(),) * 8,
        out_specs=image,
        check_vma=False,
    )
```

```python
import math

import jax
import jax.numpy as jnp
from jax import lax
from jax.experimental import pallas as pl
from jax.experimental.pallas import tpu as pltpu
from jax.sharding import PartitionSpec as P

CH = 512
HEADS = 8
GROUP = 8
FAR = (5, 4, 3, 7, 2, 6, 1)
PATCH = 8
TEMB = 128
FEAT = 192
GRID = 32
ROWS = 256
EDGE = 32
ALL = ROWS + 2 * EDGE
PLANE = 8
LINES = 8
QUADS = 4
EPS = 1e-05
MESH = pl.DeviceIdType.MESH
F32 = jnp.float32
BF16 = jnp.bfloat16
NT = (((1,), (1,)), ((), ()))


def iota(shape, dim):
    return lax.broadcasted_iota(jnp.int32, shape, dim)


def dot(a, b):
    return jnp.dot(a, b, preferred_element_type=F32)


def dot_nt(a, b):
    return lax.dot_general(a, b, NT, preferred_element_type=F32)


def pack(x):
    low = jnp.concatenate([x[16:24, :128], x[16:24, 128:]], axis=0)
    return jnp.concatenate([x[:16], low], axis=1).astype(BF16)


def unpack(y):
    y = y.astype(F32)
    low = jnp.concatenate([y[:8, 256:], y[8:, 256:]], axis=1)
    return jnp.concatenate([y[:, :256], low], axis=0)


def flat(v):
    return jnp.concatenate([v[i : i + 1] for i in range(4)], axis=1)


def sums_of(x):
    def fold(v):
        v = jnp.sum(v, axis=0, keepdims=True)
        return [v[:, 128 * i : 128 * (i + 1)] for i in range(4)]

    return jnp.concatenate(fold(x) + fold(x * x), axis=0)


def scale_shift(total, count):
    lane = iota((8, 128), 1)
    for s in (1, 2, 4, 8):
        up = pltpu.roll(total, 128 - s, axis=1)
        down = pltpu.roll(total, s, axis=1)
        total = total + jnp.where((lane & s) == 0, up, down)
    total = total / count
    mean, square = total[:4], total[4:]
    rstd = lax.rsqrt(square - mean * mean + EPS)
    shift = -mean * rstd
    return flat(rstd), flat(shift)


def kernel(
    st_h, no_h, ws, pw_h, tw_h, c1_h, c2_h, aw_h, pr_h, ow_h, early, late,
    st, no, pw, tw, c1, c2, aw, pr, ow, wqt, wvt, prt,
    hid, act, inn, blk, blkt, kbuf, vbuf, qz, att, mref, lref, big,
    stat_own, stat_in, e_own, e_in, e_tot, e_line, e_pre, e_out, e_sum, ihalo, raw,
    p_own, p_in, p_tot, p_line, p_pre, p_out,
    load, early_sem, halo_s, halo_r, stat_s, stat_r, inn_s, inn_r, gat_s, gat_r,
    ea_s, ea_r, eb_s, eb_r, ec_s, ec_r, pa_s, pa_r, pb_s, pb_r, pc_s, pc_r,
):
    step = lax.axis_index("step")
    quad = lax.axis_index("quad")
    line = step // PLANE
    spot = step % PLANE


    def at_quad(j):
        return (step, (quad + j) % QUADS)

    def spot_of(j):
        return ((spot // 2 + j // 2) % 4) * 2 + (spot + j) % 2

    def at_spot(j):
        return (line * PLANE + spot_of(j), quad)

    def at_line(j):
        return (((line + j) % LINES) * PLANE + spot, quad)

    barrier = pltpu.get_barrier_semaphore()
    peers = [at_line(j) for j in (4, 3, 5, 2, 6, 1, 7)]
    peers += [at_spot(j) for j in FAR]
    peers += [at_quad(j) for j in range(1, QUADS)]
    for peer in peers:
        pl.semaphore_signal(barrier, inc=1, device_id=peer, device_id_type=MESH)

    def send(src, dst, ss, rs, peer):
        copy = pltpu.make_async_remote_copy(
            src_ref=src, dst_ref=dst, send_sem=ss, recv_sem=rs, device_id=peer, device_id_type=MESH
        )
        copy.start()
        return copy

    loads = [
        pltpu.make_async_copy(st_h, st.at[:, pl.ds(8, 64), :], load.at[0]),
        pltpu.make_async_copy(pw_h, pw, load.at[1]),
        pltpu.make_async_copy(no_h, no, load.at[2]),
        pltpu.make_async_copy(tw_h, tw, load.at[3]),
        pltpu.make_async_copy(c1_h, c1, load.at[4]),
        pltpu.make_async_copy(c2_h, c2, load.at[5]),
        pltpu.make_async_copy(aw_h, aw, load.at[6]),
        pltpu.make_async_copy(pr_h, pr, load.at[7]),
        pltpu.make_async_copy(ow_h, ow, load.at[8]),
    ]
    for item in loads:
        item.start()
    feat = iota((FEAT, ROWS), 0)
    pixel = iota((FEAT, ROWS), 1)
    diag = (feat & 7) == (pixel & 7)
    spread = (iota((FEAT, 24), 0) >> 3 == iota((FEAT, 24), 1)).astype(F32).astype(BF16)
    big[...] = (iota((ROWS, 8 * ROWS), 0) == iota((ROWS, 8 * ROWS), 1) >> 3).astype(F32).astype(BF16)

    def on_diag(v):
        pieces = [v[:, i : i + ROWS] for i in range(0, v.shape[1], ROWS)]
        return jnp.concatenate([jnp.where(diag, piece, 0.0) for piece in pieces], axis=1).astype(BF16)


    loads[0].wait()
    loads[1].wait()

    inside = [st[:, pl.ds(8 * r, 8), :].reshape(24, ROWS) for r in range(1, 9)]
    wide = dot(spread, jnp.concatenate(inside, axis=1).astype(BF16))
    patches = dot_nt(big[...], on_diag(wide)).astype(BF16)
    hid[pl.ds(EDGE, ROWS), :] = dot(patches, pw[...])
    own = pl.ds(EDGE, ROWS)
    stat_own[0] = sums_of(hid[own, :])

    pl.semaphore_wait(barrier, len(peers))
    halo = [
        send(st.at[:, pl.ds(64, 8), :], st.at[:, pl.ds(0, 8), :], halo_s.at[0], halo_r.at[0], at_quad(1)),
        send(st.at[:, pl.ds(8, 8), :], st.at[:, pl.ds(72, 8), :], halo_s.at[1], halo_r.at[1], at_quad(3)),
    ]


    def share_sums(k):
        return [
            send(stat_own.at[k], stat_in.at[k, j - 1], stat_s.at[3 * k + j - 1], stat_r.at[3 * k + j - 1], at_quad(j))
            for j in range(1, QUADS)
        ]

    def total_sums(k, copies):
        total = stat_own[k]
        for j, copy in enumerate(copies):
            copy.wait()
            total = total + stat_in[k, j]
        return scale_shift(total, float(QUADS * ROWS * CH // 32))

    stats = share_sums(0)

    time = 999 - ws[0] - step
    when = jnp.full((8, 128), time.astype(F32))
    place = iota((8, 128), 0) * 128 + iota((8, 128), 1)
    beta_all = 0.0001 + (0.02 - 0.0001) * place.astype(F32) / 999.0
    log_all = jnp.where(place <= time, jnp.log1p(-beta_all), 0.0)
    log_now = jnp.sum(jnp.sum(log_all, axis=1, keepdims=True), axis=0, keepdims=True)
    beta = (0.0001 + (0.02 - 0.0001) * when / 999.0)[:1, :1]
    keep = jnp.exp(log_now)
    root = lax.rsqrt(1.0 - beta)
    of_state = root - 1.0
    of_noise = jnp.sqrt(beta)
    of_pred = -beta * root * lax.rsqrt(1.0 - keep)
    half = TEMB // 2
    lane = iota((8, TEMB), 1)
    angle = when * jnp.exp(-math.log(10000.0) * (lane & (half - 1)).astype(F32) / half)
    embed = jnp.where(lane < half, jnp.cos(angle), jnp.sin(angle)).astype(BF16)
    loads[3].wait()
    embed = dot(embed, tw[...])[:1]
    time_scale, time_shift = 1.0 + embed[:, :CH], embed[:, CH:]

    loads[2].wait()
    head = jnp.where(step == 0, 1.0, 0.0)

    @pl.loop(0, 8)
    def _(r):
        here = st[:, pl.ds(pl.multiple_of(8 * r + 8, 8), 8), :].reshape(24, ROWS)
        push = no[:, pl.ds(pl.multiple_of(8 * r, 8), 8), :].reshape(24, ROWS)
        e_own[r] = (of_state + head) * here + of_noise * push

    def scatter(own_ref, in_ref, ss, rs):
        return [
            send(own_ref.at[spot_of(j)], in_ref.at[spot], ss.at[j], rs.at[j], at_spot(j))
            for j in FAR
        ]

    def to_lines(tot, line_in, ss, rs, start):
        for j in range(1, LINES):
            copy = pltpu.make_async_remote_copy(
                src_ref=tot, dst_ref=line_in.at[j], send_sem=ss.at[j], recv_sem=rs.at[j],
                device_id=at_line(j), device_id_type=MESH,
            )

            @pl.when(line + j < LINES)
            def _():
                if start:
                    copy.start()
                else:
                    copy.wait_send()

            if not start:

                @pl.when(line >= j)
                def _():
                    copy.wait_recv()

    def lines_sum(line_in, shape, load_one):
        base = jnp.zeros(shape, F32)
        for j in range(1, LINES):
            base = base + jnp.where(line >= j, load_one(line_in, j), 0.0)
        return base

    def back(pre, out_ref, ss, rs):
        return [
            send(pre.at[spot_of(j)], out_ref.at[spot], ss.at[j], rs.at[j], at_spot(j))
            for j in FAR
        ]

    early_a = scatter(e_own, e_in, ea_s, ea_r)

    for item in halo:
        item.wait()
    outer = [st[:, pl.ds(8 * r, 8), :].reshape(24, ROWS) for r in (0, 9)]
    wide = on_diag(dot(spread, jnp.concatenate(outer, axis=1).astype(BF16)))
    patches = dot_nt(big[0 : 2 * GRID, 0 : 2 * ROWS], wide).astype(BF16)
    edge_rows = dot(patches, pw[...])
    hid[pl.ds(0, EDGE), :] = edge_rows[:EDGE]
    hid[pl.ds(ALL - EDGE, EDGE), :] = edge_rows[EDGE:]
    scale, shift = total_sums(0, stats)

    def activate(source, gain, bias):
        @pl.loop(0, 10)
        def _(r):
            where = pl.ds(pl.multiple_of(GRID * r, GRID), GRID)
            x = source[where, :] * gain + bias
            outside = ((quad == 0) & (r == 0)) | ((quad == QUADS - 1) & (r == 9))
            x = x * (jnp.tanh(0.5 * x) + 1.0) * jnp.where(outside, 0.0, 0.5)
            col = iota((GRID, CH), 0)
            act[0, where, :] = jnp.where(col == 0, 0.0, pltpu.roll(x, 1, axis=0)).astype(BF16)
            act[1, where, :] = x.astype(BF16)
            act[2, where, :] = jnp.where(col == GRID - 1, 0.0, pltpu.roll(x, GRID - 1, axis=0)).astype(BF16)

    def convolve(weight, n):
        total = None
        for row in range(3):
            for col in range(3):
                term = dot(
                    act[col, pl.ds(GRID * row, ROWS), :],
                    weight[pl.ds((3 * row + col) * CH, CH), pl.ds(256 * n, 256)],
                )
                total = term if total is None else total + term
        return total

    activate(hid, scale, shift)
    loads[4].wait()
    for n in range(2):
        inn[own, pl.ds(256 * n, 256)] = convolve(c1, n)
    stat_own[1] = sums_of(inn[own, :])
    stats = share_sums(1)
    middle = flat(stat_own[1]) / ROWS
    ihalo[0] = (inn[pl.ds(ROWS, EDGE), :] - middle).astype(BF16)
    ihalo[1] = (inn[pl.ds(EDGE, EDGE), :] - middle).astype(BF16)
    edges = [
        send(ihalo.at[0], ihalo.at[2], inn_s.at[0], inn_r.at[0], at_quad(1)),
        send(ihalo.at[1], ihalo.at[3], inn_s.at[1], inn_r.at[1], at_quad(3)),
    ]

    for item in early_a:
        item.wait()
    e_in[spot] = e_own[spot]
    run = jnp.zeros((24, ROWS), F32)
    for d in range(PLANE):
        e_pre[d] = run
        run = run + e_in[d]
    e_tot[...] = run
    to_lines(e_tot, e_line, eb_s, eb_r, True)
    loads[6].wait()
    wqt[...] = aw[:, :CH].T

    scale, shift = total_sums(1, stats)
    for item in edges:
        item.wait()
    inn[pl.ds(0, EDGE), :] = ihalo[2].astype(F32) + flat(stat_in[1, 0]) / ROWS
    inn[pl.ds(ALL - EDGE, EDGE), :] = ihalo[3].astype(F32) + flat(stat_in[1, 2]) / ROWS
    activate(inn, scale * time_scale, shift * time_scale + time_shift)
    loads[5].wait()
    for n in range(2):
        lanes = pl.ds(256 * n, 256)
        blk[:, lanes] = hid[own, lanes] + convolve(c2, n)
    stat_own[2] = sums_of(blk[...])
    stats = share_sums(2)
    raw[0] = (blk[...] - flat(stat_own[2]) / ROWS).astype(BF16)
    low, high = pl.ds(0, 128), pl.ds(128, 128)
    low_r = send(raw.at[0, low], raw.at[1, low], gat_s.at[0], gat_r.at[0], at_quad(1))
    high_l = send(raw.at[0, high], raw.at[2, high], gat_s.at[1], gat_r.at[1], at_quad(3))
    high_r = send(raw.at[0, high], raw.at[1, high], gat_s.at[2], gat_r.at[2], at_quad(1))
    low_l = send(raw.at[0, low], raw.at[2, low], gat_s.at[3], gat_r.at[3], at_quad(3))


    wvt[...] = aw[:, 2 * CH :].T

    scale, shift = total_sums(2, stats)
    normed = (blk[...] * scale + shift).astype(BF16)
    queries = dot_nt(wqt[...], normed).astype(BF16)
    upper = iota((128, ROWS), 0) < 64
    for p in range(4):
        pair = queries[128 * p : 128 * (p + 1)]
        qz[2 * p] = jnp.where(upper, pair, jnp.zeros_like(pair))
        qz[2 * p + 1] = jnp.where(upper, jnp.zeros_like(pair), pair)
    sharp = math.log2(math.e) / 8.0

    def attend(slots, normed=None):
        first, keys = slots == (0,), len(slots) * ROWS
        for i, slot in enumerate(slots):
            if slot > 0:
                offset = flat(stat_in[2, (0, 2, 1)[slot - 1]]) / ROWS * scale + shift
                normed = (raw[slot].astype(F32) * scale + offset).astype(BF16)
            kbuf[pl.ds(ROWS * i, ROWS), :] = dot(normed, aw[:, CH : 2 * CH]).astype(BF16)
            vbuf[:, pl.ds(ROWS * i, ROWS)] = dot_nt(wvt[...], normed).astype(BF16)

        def some(base):
            scores, most, weights, total = {}, {}, {}, {}
            for g in range(GROUP):
                h = base + g
                pair = pl.ds(pl.multiple_of(128 * (h // 2), 128), 128)
                scores[g] = dot(kbuf[0:keys, pair], qz[h])
            for g in range(GROUP):
                h = base + g
                most[g] = jnp.max(scores[g], axis=0, keepdims=True)
                if not first:
                    most[g] = jnp.maximum(most[g], mref[h])
                e = jnp.exp2((scores[g] - most[g]) * sharp)
                total[g] = jnp.sum(e, axis=0, keepdims=True)
                weights[g] = e.astype(BF16)
            for g in range(GROUP):
                h = base + g
                rows = pl.ds(pl.multiple_of(64 * h, 64), 64)
                value = dot(vbuf[rows, 0:keys], weights[g])
                if not first:
                    fade = jnp.exp2((mref[h] - most[g]) * sharp)
                    total[g] = total[g] + lref[h] * fade
                    value = value + att[rows, :] * fade
                mref[h] = most[g]
                lref[h] = total[g]
                att[rows, :] = value

        if GROUP == HEADS:
            some(0)
        else:
            pl.loop(0, HEADS // GROUP)(lambda i: some(i * GROUP))

    attend((0,), normed)
    low_r.wait_recv()
    pass_r = send(raw.at[1, low], raw.at[3, low], gat_s.at[4], gat_r.at[4], at_quad(1))
    high_l.wait_recv()
    pass_l = send(raw.at[2, high], raw.at[3, high], gat_s.at[5], gat_r.at[5], at_quad(3))
    loads[7].wait()
    loads[8].wait()
    prt[...] = pr[...].T
    blkt[...] = blk[...].T
    to_lines(e_tot, e_line, eb_s, eb_r, False)
    base = lines_sum(e_line, (24, ROWS), lambda ref, j: ref[j])
    for d in range(PLANE):
        e_pre[d] = e_pre[d] + base
    early_c = back(e_pre, e_out, ec_s, ec_r)
    high_r.wait_recv()
    low_l.wait_recv()
    attend((1, 2))
    pass_r.wait_recv()
    pass_l.wait_recv()
    attend((3,))
    for h in range(HEADS):
        rows = pl.ds(64 * h, 64)
        att[rows, :] = att[rows, :] / lref[h]

    mixed = blkt[...] + dot(prt[...], att[...].astype(BF16))
    predicted = (dot(ow[...], mixed.astype(BF16)) * of_pred).astype(BF16)
    wide = dot(predicted, big[...])
    wide = lax.dot_general(spread, on_diag(wide), (((0,), (0,)), ((), ())), preferred_element_type=F32)
    for r in range(8):
        p_own[r] = pack(wide[:, 256 * r : 256 * (r + 1)])
    late_a = scatter(p_own, p_in, pa_s, pa_r)
    p_in[spot] = p_own[spot]
    for item in late_a:
        item.wait()
    run = jnp.zeros((16, 384), F32)
    runs = []
    for d in range(PLANE):
        runs.append(run)
        run = run + p_in[d].astype(F32)
    p_tot[...] = run.astype(BF16)
    to_lines(p_tot, p_line, pb_s, pb_r, True)
    for item in early_c:
        item.wait()
    e_out[spot] = e_pre[spot]
    for r in range(8):
        e_sum[:, pl.ds(8 * r, 8), :] = (e_out[r] + e_own[r]).reshape(3, 8, ROWS)
    early_copy = pltpu.make_async_copy(e_sum, early, early_sem.at[0])
    early_copy.start()
    to_lines(p_tot, p_line, pb_s, pb_r, False)
    base = lines_sum(p_line, (16, 384), lambda ref, j: ref[j].astype(F32))
    for d in range(PLANE):
        p_pre[d] = runs[d] + base
    late_c = back(p_pre, p_out, pc_s, pc_r)
    p_out[spot] = p_pre[spot]
    for item in late_c:
        item.wait()
    for r in range(8):
        late[:, pl.ds(8 * r, 8), :] = (unpack(p_out[r]) + unpack(p_own[r])).reshape(3, 8, ROWS)
    early_copy.wait()
    for item in (low_r, high_l, high_r, low_l, pass_r, pass_l):
        item.wait_send()


def body(states, noise, ws, pw, tw, c1, c2, aw, pr, ow):
    dma = pltpu.SemaphoreType.DMA
    vmem = pltpu.VMEM
    anyhow = pl.BlockSpec(memory_space=pl.ANY)
    chunk, small = (24, ROWS), (16, 384)
    scratch = [
        vmem((3, 80, 256), F32), vmem((3, 64, 256), F32),
        vmem((FEAT, CH), BF16), vmem((TEMB, 2 * CH), BF16),
        vmem((9 * CH, CH), BF16), vmem((9 * CH, CH), BF16),
        vmem((CH, 3 * CH), BF16), vmem((CH, CH), BF16), vmem((FEAT, CH), BF16),
        vmem((CH, CH), BF16), vmem((CH, CH), BF16), vmem((CH, CH), BF16),
        vmem((ALL, CH), F32), vmem((3, ALL, CH), BF16), vmem((ALL, CH), F32),
        vmem((ROWS, CH), F32), vmem((CH, ROWS), F32),
        vmem((2 * ROWS, CH), BF16), vmem((CH, 2 * ROWS), BF16),
        vmem((8, 128, ROWS), BF16), vmem((CH, ROWS), F32),
        vmem((8, 1, ROWS), F32), vmem((8, 1, ROWS), F32), vmem((ROWS, 8 * ROWS), BF16),
        vmem((3, 8, 128), F32), vmem((3, 3, 8, 128), F32),
        vmem((8,) + chunk, F32), vmem((8,) + chunk, F32), vmem(chunk, F32), vmem((8,) + chunk, F32),
        vmem((8,) + chunk, F32), vmem((8,) + chunk, F32),
        vmem((3, 64, 256), F32), vmem((4, EDGE, CH), BF16), vmem((4, ROWS, CH), BF16),
        vmem((8,) + small, BF16), vmem((8,) + small, BF16), vmem(small, BF16), vmem((8,) + small, BF16),
        vmem((8,) + small, F32), vmem((8,) + small, F32),
        dma((9,)), dma((1,)), dma((2,)), dma((2,)), dma((9,)), dma((9,)), dma((2,)), dma((2,)), dma((6,)), dma((6,)),
    ] + [dma((8,)) for _ in range(12)]
    early, late = pl.pallas_call(
        kernel,
        out_shape=[jax.ShapeDtypeStruct((3, 64, 256), F32)] * 2,
        in_specs=[anyhow, anyhow, pl.BlockSpec(memory_space=pltpu.SMEM)] + [anyhow] * 7,
        out_specs=[anyhow, pl.BlockSpec(memory_space=pltpu.VMEM)],
        scratch_shapes=scratch,
        compiler_params=pltpu.CompilerParams(
            collective_id=0, has_side_effects=True, vmem_limit_bytes=56 * 1024 * 1024
        ),
    )(
        states[0], noise[0], ws, pw, tw,
        c1.reshape(9 * CH, CH), c2.reshape(9 * CH, CH), aw, pr, ow.T,
    )
    return (early + late)[None]


def solution(mesh):
    image = P("step", None, "quad", None)
    return jax.shard_map(
        body,
        mesh=mesh,
        in_specs=(image, image) + (P(),) * 8,
        out_specs=image,
        check_vma=False,
    )
```

```python
import math

import jax
import jax.numpy as jnp
from jax import lax
from jax.experimental import pallas as pl
from jax.experimental.pallas import tpu as pltpu
from jax.sharding import PartitionSpec as P

CH = 512
HEADS = 8
GROUP = 8
FAR = (5, 4, 3, 7, 2, 6, 1)
PATCH = 8
TEMB = 128
FEAT = 192
GRID = 32
ROWS = 256
EDGE = 32
ALL = ROWS + 2 * EDGE
PLANE = 8
LINES = 8
QUADS = 4
EPS = 1e-05
MESH = pl.DeviceIdType.MESH
F32 = jnp.float32
BF16 = jnp.bfloat16
NT = (((1,), (1,)), ((), ()))


def iota(shape, dim):
    return lax.broadcasted_iota(jnp.int32, shape, dim)


def dot(a, b):
    return jnp.dot(a, b, preferred_element_type=F32)


def dot_nt(a, b):
    return lax.dot_general(a, b, NT, preferred_element_type=F32)


def pack(x):
    low = jnp.concatenate([x[16:24, :128], x[16:24, 128:]], axis=0)
    return jnp.concatenate([x[:16], low], axis=1).astype(BF16)


def unpack(y):
    y = y.astype(F32)
    low = jnp.concatenate([y[:8, 256:], y[8:, 256:]], axis=1)
    return jnp.concatenate([y[:, :256], low], axis=0)


def flat(v):
    return jnp.concatenate([v[i : i + 1] for i in range(4)], axis=1)


def sums_of(x):
    def fold(v):
        v = jnp.sum(v, axis=0, keepdims=True)
        return [v[:, 128 * i : 128 * (i + 1)] for i in range(4)]

    return jnp.concatenate(fold(x) + fold(x * x), axis=0)


def scale_shift(total, count):
    lane = iota((8, 128), 1)
    for s in (1, 2, 4, 8):
        up = pltpu.roll(total, 128 - s, axis=1)
        down = pltpu.roll(total, s, axis=1)
        total = total + jnp.where((lane & s) == 0, up, down)
    total = total / count
    mean, square = total[:4], total[4:]
    rstd = lax.rsqrt(square - mean * mean + EPS)
    shift = -mean * rstd
    return flat(rstd), flat(shift)


def kernel(
    st_h, no_h, ws, pw_h, tw_h, c1_h, c2_h, aw_h, pr_h, ow_h, early, late,
    st, no, pw, tw, c1, c2, aw, pr, ow, wqt, wvt, prt,
    hid, act, inn, blk, blkt, kbuf, vbuf, qz, att, mref, lref, big,
    stat_own, stat_in, e_own, e_in, e_tot, e_line, e_pre, e_out, e_sum, ihalo, raw,
    p_own, p_in, p_tot, p_line, p_pre, p_out,
    load, early_sem, halo_s, halo_r, stat_s, stat_r, inn_s, inn_r, gat_s, gat_r,
    ea_s, ea_r, eb_s, eb_r, ec_s, ec_r, pa_s, pa_r, pb_s, pb_r, pc_s, pc_r,
):
    step = lax.axis_index("step")
    quad = lax.axis_index("quad")
    line = step // PLANE
    spot = step % PLANE


    def at_quad(j):
        return (step, (quad + j) % QUADS)

    def spot_of(j):
        return ((spot // 2 + j // 2) % 4) * 2 + (spot + j) % 2

    def at_spot(j):
        return (line * PLANE + spot_of(j), quad)

    def at_line(j):
        return (((line + j) % LINES) * PLANE + spot, quad)

    barrier = pltpu.get_barrier_semaphore()
    peers = [at_line(j) for j in (4, 3, 5, 2, 6, 1, 7)]
    peers += [at_spot(j) for j in FAR]
    peers += [at_quad(j) for j in range(1, QUADS)]
    for peer in peers:
        pl.semaphore_signal(barrier, inc=1, device_id=peer, device_id_type=MESH)

    def send(src, dst, ss, rs, peer):
        copy = pltpu.make_async_remote_copy(
            src_ref=src, dst_ref=dst, send_sem=ss, recv_sem=rs, device_id=peer, device_id_type=MESH
        )
        copy.start()
        return copy

    loads = [
        pltpu.make_async_copy(st_h, st.at[:, pl.ds(8, 64), :], load.at[0]),
        pltpu.make_async_copy(pw_h, pw, load.at[1]),
        pltpu.make_async_copy(no_h, no, load.at[2]),
        pltpu.make_async_copy(tw_h, tw, load.at[3]),
        pltpu.make_async_copy(c1_h, c1, load.at[4]),
        pltpu.make_async_copy(c2_h, c2, load.at[5]),
        pltpu.make_async_copy(aw_h, aw, load.at[6]),
        pltpu.make_async_copy(pr_h, pr, load.at[7]),
        pltpu.make_async_copy(ow_h, ow, load.at[8]),
    ]
    for item in loads:
        item.start()
    feat = iota((FEAT, ROWS), 0)
    pixel = iota((FEAT, ROWS), 1)
    diag = (feat & 7) == (pixel & 7)
    spread = (iota((FEAT, 24), 0) >> 3 == iota((FEAT, 24), 1)).astype(F32).astype(BF16)
    big[...] = (iota((ROWS, 8 * ROWS), 0) == iota((ROWS, 8 * ROWS), 1) >> 3).astype(F32).astype(BF16)

    def on_diag(v):
        pieces = [v[:, i : i + ROWS] for i in range(0, v.shape[1], ROWS)]
        return jnp.concatenate([jnp.where(diag, piece, 0.0) for piece in pieces], axis=1).astype(BF16)


    loads[0].wait()
    loads[1].wait()

    inside = [st[:, pl.ds(8 * r, 8), :].reshape(24, ROWS) for r in range(1, 9)]
    wide = dot(spread, jnp.concatenate(inside, axis=1).astype(BF16))
    patches = dot_nt(big[...], on_diag(wide)).astype(BF16)
    hid[pl.ds(EDGE, ROWS), :] = dot(patches, pw[...])
    own = pl.ds(EDGE, ROWS)
    stat_own[0] = sums_of(hid[own, :])

    pl.semaphore_wait(barrier, len(peers))
    halo = [
        send(st.at[:, pl.ds(64, 8), :], st.at[:, pl.ds(0, 8), :], halo_s.at[0], halo_r.at[0], at_quad(1)),
        send(st.at[:, pl.ds(8, 8), :], st.at[:, pl.ds(72, 8), :], halo_s.at[1], halo_r.at[1], at_quad(3)),
    ]


    def share_sums(k):
        return [
            send(stat_own.at[k], stat_in.at[k, j - 1], stat_s.at[3 * k + j - 1], stat_r.at[3 * k + j - 1], at_quad(j))
            for j in range(1, QUADS)
        ]

    def total_sums(k, copies):
        total = stat_own[k]
        for j, copy in enumerate(copies):
            copy.wait()
            total = total + stat_in[k, j]
        return scale_shift(total, float(QUADS * ROWS * CH // 32))

    stats = share_sums(0)

    time = 999 - ws[0] - step
    when = jnp.full((8, 128), time.astype(F32))
    place = iota((8, 128), 0) * 128 + iota((8, 128), 1)
    beta_all = 0.0001 + (0.02 - 0.0001) * place.astype(F32) / 999.0
    log_all = jnp.where(place <= time, jnp.log1p(-beta_all), 0.0)
    log_now = jnp.sum(jnp.sum(log_all, axis=1, keepdims=True), axis=0, keepdims=True)
    beta = (0.0001 + (0.02 - 0.0001) * when / 999.0)[:1, :1]
    keep = jnp.exp(log_now)
    root = lax.rsqrt(1.0 - beta)
    of_state = root - 1.0
    of_noise = jnp.sqrt(beta)
    of_pred = -beta * root * lax.rsqrt(1.0 - keep)
    half = TEMB // 2
    lane = iota((8, TEMB), 1)
    angle = when * jnp.exp(-math.log(10000.0) * (lane & (half - 1)).astype(F32) / half)
    embed = jnp.where(lane < half, jnp.cos(angle), jnp.sin(angle)).astype(BF16)
    loads[3].wait()
    embed = dot(embed, tw[...])[:1]
    time_scale, time_shift = 1.0 + embed[:, :CH], embed[:, CH:]

    loads[2].wait()
    head = jnp.where(step == 0, 1.0, 0.0)

    @pl.loop(0, 8)
    def _(r):
        here = st[:, pl.ds(pl.multiple_of(8 * r + 8, 8), 8), :].reshape(24, ROWS)
        push = no[:, pl.ds(pl.multiple_of(8 * r, 8), 8), :].reshape(24, ROWS)
        e_own[r] = (of_state + head) * here + of_noise * push

    def scatter(own_ref, in_ref, ss, rs):
        return [
            send(own_ref.at[spot_of(j)], in_ref.at[spot], ss.at[j], rs.at[j], at_spot(j))
            for j in FAR
        ]

    def to_lines(tot, line_in, ss, rs, start):
        for j in range(1, LINES):
            copy = pltpu.make_async_remote_copy(
                src_ref=tot, dst_ref=line_in.at[j], send_sem=ss.at[j], recv_sem=rs.at[j],
                device_id=at_line(j), device_id_type=MESH,
            )

            @pl.when(line + j < LINES)
            def _():
                if start:
                    copy.start()
                else:
                    copy.wait_send()

            if not start:

                @pl.when(line >= j)
                def _():
                    copy.wait_recv()

    def lines_sum(line_in, shape, load_one):
        base = jnp.zeros(shape, F32)
        for j in range(1, LINES):
            base = base + jnp.where(line >= j, load_one(line_in, j), 0.0)
        return base

    def back(pre, out_ref, ss, rs):
        return [
            send(pre.at[spot_of(j)], out_ref.at[spot], ss.at[j], rs.at[j], at_spot(j))
            for j in FAR
        ]

    early_a = scatter(e_own, e_in, ea_s, ea_r)

    for item in halo:
        item.wait()
    outer = [st[:, pl.ds(8 * r, 8), :].reshape(24, ROWS) for r in (0, 9)]
    wide = on_diag(dot(spread, jnp.concatenate(outer, axis=1).astype(BF16)))
    patches = dot_nt(big[0 : 2 * GRID, 0 : 2 * ROWS], wide).astype(BF16)
    edge_rows = dot(patches, pw[...])
    hid[pl.ds(0, EDGE), :] = edge_rows[:EDGE]
    hid[pl.ds(ALL - EDGE, EDGE), :] = edge_rows[EDGE:]
    scale, shift = total_sums(0, stats)

    def activate(source, gain, bias):
        @pl.loop(0, 10)
        def _(r):
            where = pl.ds(pl.multiple_of(GRID * r, GRID), GRID)
            x = source[where, :] * gain + bias
            outside = ((quad == 0) & (r == 0)) | ((quad == QUADS - 1) & (r == 9))
            x = x * (jnp.tanh(0.5 * x) + 1.0) * jnp.where(outside, 0.0, 0.5)
            col = iota((GRID, CH), 0)
            act[0, where, :] = jnp.where(col == 0, 0.0, pltpu.roll(x, 1, axis=0)).astype(BF16)
            act[1, where, :] = x.astype(BF16)
            act[2, where, :] = jnp.where(col == GRID - 1, 0.0, pltpu.roll(x, GRID - 1, axis=0)).astype(BF16)

    def convolve(weight, n):
        total = None
        for row in range(3):
            for col in range(3):
                term = dot(
                    act[col, pl.ds(GRID * row, ROWS), :],
                    weight[pl.ds((3 * row + col) * CH, CH), pl.ds(256 * n, 256)],
                )
                total = term if total is None else total + term
        return total

    activate(hid, scale, shift)
    loads[4].wait()
    for n in range(2):
        inn[own, pl.ds(256 * n, 256)] = convolve(c1, n)
    stat_own[1] = sums_of(inn[own, :])
    stats = share_sums(1)
    middle = flat(stat_own[1]) / ROWS
    ihalo[0] = (inn[pl.ds(ROWS, EDGE), :] - middle).astype(BF16)
    ihalo[1] = (inn[pl.ds(EDGE, EDGE), :] - middle).astype(BF16)
    edges = [
        send(ihalo.at[0], ihalo.at[2], inn_s.at[0], inn_r.at[0], at_quad(1)),
        send(ihalo.at[1], ihalo.at[3], inn_s.at[1], inn_r.at[1], at_quad(3)),
    ]

    for item in early_a:
        item.wait()
    e_in[spot] = e_own[spot]
    run = jnp.zeros((24, ROWS), F32)
    for d in range(PLANE):
        e_pre[d] = run
        run = run + e_in[d]
    e_tot[...] = run
    to_lines(e_tot, e_line, eb_s, eb_r, True)
    loads[6].wait()
    wqt[...] = aw[:, :CH].T

    scale, shift = total_sums(1, stats)
    for item in edges:
        item.wait()
    inn[pl.ds(0, EDGE), :] = ihalo[2].astype(F32) + flat(stat_in[1, 0]) / ROWS
    inn[pl.ds(ALL - EDGE, EDGE), :] = ihalo[3].astype(F32) + flat(stat_in[1, 2]) / ROWS
    activate(inn, scale * time_scale, shift * time_scale + time_shift)
    loads[5].wait()
    for n in range(2):
        lanes = pl.ds(256 * n, 256)
        blk[:, lanes] = hid[own, lanes] + convolve(c2, n)
    stat_own[2] = sums_of(blk[...])
    stats = share_sums(2)
    raw[0] = (blk[...] - flat(stat_own[2]) / ROWS).astype(BF16)
    low, high = pl.ds(0, 128), pl.ds(128, 128)
    low_r, high_l = [], []
    for i in range(2):
        a, b = pl.ds(64 * i, 64), pl.ds(128 + 64 * i, 64)
        low_r.append(send(raw.at[0, a], raw.at[1, a], gat_s.at[i], gat_r.at[i], at_quad(1)))
        high_l.append(send(raw.at[0, b], raw.at[2, b], gat_s.at[2 + i], gat_r.at[2 + i], at_quad(3)))
    high_r = send(raw.at[0, high], raw.at[1, high], gat_s.at[4], gat_r.at[4], at_quad(1))
    low_l = send(raw.at[0, low], raw.at[2, low], gat_s.at[5], gat_r.at[5], at_quad(3))


    wvt[...] = aw[:, 2 * CH :].T

    scale, shift = total_sums(2, stats)
    pass_r, pass_l = [], []

    def forward(i):
        a, b = pl.ds(64 * i, 64), pl.ds(128 + 64 * i, 64)
        low_r[i].wait_recv()
        pass_r.append(send(raw.at[1, a], raw.at[3, a], gat_s.at[6 + i], gat_r.at[6 + i], at_quad(1)))
        high_l[i].wait_recv()
        pass_l.append(send(raw.at[2, b], raw.at[3, b], gat_s.at[8 + i], gat_r.at[8 + i], at_quad(3)))

    forward(0)
    normed = (blk[...] * scale + shift).astype(BF16)
    queries = dot_nt(wqt[...], normed).astype(BF16)
    upper = iota((128, ROWS), 0) < 64
    for p in range(4):
        pair = queries[128 * p : 128 * (p + 1)]
        qz[2 * p] = jnp.where(upper, pair, jnp.zeros_like(pair))
        qz[2 * p + 1] = jnp.where(upper, jnp.zeros_like(pair), pair)
    sharp = math.log2(math.e) / 8.0

    def attend(slots, normed=None):
        first, keys = slots == (0,), len(slots) * ROWS
        for i, slot in enumerate(slots):
            if slot > 0:
                offset = flat(stat_in[2, (0, 2, 1)[slot - 1]]) / ROWS * scale + shift
                normed = (raw[slot].astype(F32) * scale + offset).astype(BF16)
            kbuf[pl.ds(ROWS * i, ROWS), :] = dot(normed, aw[:, CH : 2 * CH]).astype(BF16)
            vbuf[:, pl.ds(ROWS * i, ROWS)] = dot_nt(wvt[...], normed).astype(BF16)

        def some(base):
            scores, most, weights, total = {}, {}, {}, {}
            for g in range(GROUP):
                h = base + g
                pair = pl.ds(pl.multiple_of(128 * (h // 2), 128), 128)
                scores[g] = dot(kbuf[0:keys, pair], qz[h])
            for g in range(GROUP):
                h = base + g
                most[g] = jnp.max(scores[g], axis=0, keepdims=True)
                if not first:
                    most[g] = jnp.maximum(most[g], mref[h])
                e = jnp.exp2((scores[g] - most[g]) * sharp)
                total[g] = jnp.sum(e, axis=0, keepdims=True)
                weights[g] = e.astype(BF16)
            for g in range(GROUP):
                h = base + g
                rows = pl.ds(pl.multiple_of(64 * h, 64), 64)
                value = dot(vbuf[rows, 0:keys], weights[g])
                if not first:
                    fade = jnp.exp2((mref[h] - most[g]) * sharp)
                    total[g] = total[g] + lref[h] * fade
                    value = value + att[rows, :] * fade
                mref[h] = most[g]
                lref[h] = total[g]
                att[rows, :] = value

        if GROUP == HEADS:
            some(0)
        else:
            pl.loop(0, HEADS // GROUP)(lambda i: some(i * GROUP))

    forward(1)
    attend((0,), normed)
    loads[7].wait()
    loads[8].wait()
    prt[...] = pr[...].T
    blkt[...] = blk[...].T
    to_lines(e_tot, e_line, eb_s, eb_r, False)
    base = lines_sum(e_line, (24, ROWS), lambda ref, j: ref[j])
    for d in range(PLANE):
        e_pre[d] = e_pre[d] + base
    early_c = back(e_pre, e_out, ec_s, ec_r)
    high_r.wait_recv()
    low_l.wait_recv()
    attend((1, 2))
    for item in pass_r + pass_l:
        item.wait_recv()
    attend((3,))
    for h in range(HEADS):
        rows = pl.ds(64 * h, 64)
        att[rows, :] = att[rows, :] / lref[h]

    mixed = blkt[...] + dot(prt[...], att[...].astype(BF16))
    predicted = (dot(ow[...], mixed.astype(BF16)) * of_pred).astype(BF16)
    wide = dot(predicted, big[...])
    wide = lax.dot_general(spread, on_diag(wide), (((0,), (0,)), ((), ())), preferred_element_type=F32)
    for r in range(8):
        p_own[r] = pack(wide[:, 256 * r : 256 * (r + 1)])
    late_a = scatter(p_own, p_in, pa_s, pa_r)
    p_in[spot] = p_own[spot]
    for item in late_a:
        item.wait()
    run = jnp.zeros((16, 384), F32)
    runs = []
    for d in range(PLANE):
        runs.append(run)
        run = run + p_in[d].astype(F32)
    p_tot[...] = run.astype(BF16)
    to_lines(p_tot, p_line, pb_s, pb_r, True)
    for item in early_c:
        item.wait()
    e_out[spot] = e_pre[spot]
    for r in range(8):
        e_sum[:, pl.ds(8 * r, 8), :] = (e_out[r] + e_own[r]).reshape(3, 8, ROWS)
    early_copy = pltpu.make_async_copy(e_sum, early, early_sem.at[0])
    early_copy.start()
    to_lines(p_tot, p_line, pb_s, pb_r, False)
    base = lines_sum(p_line, (16, 384), lambda ref, j: ref[j].astype(F32))
    for d in range(PLANE):
        p_pre[d] = runs[d] + base
    late_c = back(p_pre, p_out, pc_s, pc_r)
    p_out[spot] = p_pre[spot]
    for item in late_c:
        item.wait()
    for r in range(8):
        late[:, pl.ds(8 * r, 8), :] = (unpack(p_out[r]) + unpack(p_own[r])).reshape(3, 8, ROWS)
    early_copy.wait()
    for item in low_r + high_l + [high_r, low_l] + pass_r + pass_l:
        item.wait_send()


def body(states, noise, ws, pw, tw, c1, c2, aw, pr, ow):
    dma = pltpu.SemaphoreType.DMA
    vmem = pltpu.VMEM
    anyhow = pl.BlockSpec(memory_space=pl.ANY)
    chunk, small = (24, ROWS), (16, 384)
    scratch = [
        vmem((3, 80, 256), F32), vmem((3, 64, 256), F32),
        vmem((FEAT, CH), BF16), vmem((TEMB, 2 * CH), BF16),
        vmem((9 * CH, CH), BF16), vmem((9 * CH, CH), BF16),
        vmem((CH, 3 * CH), BF16), vmem((CH, CH), BF16), vmem((FEAT, CH), BF16),
        vmem((CH, CH), BF16), vmem((CH, CH), BF16), vmem((CH, CH), BF16),
        vmem((ALL, CH), F32), vmem((3, ALL, CH), BF16), vmem((ALL, CH), F32),
        vmem((ROWS, CH), F32), vmem((CH, ROWS), F32),
        vmem((2 * ROWS, CH), BF16), vmem((CH, 2 * ROWS), BF16),
        vmem((8, 128, ROWS), BF16), vmem((CH, ROWS), F32),
        vmem((8, 1, ROWS), F32), vmem((8, 1, ROWS), F32), vmem((ROWS, 8 * ROWS), BF16),
        vmem((3, 8, 128), F32), vmem((3, 3, 8, 128), F32),
        vmem((8,) + chunk, F32), vmem((8,) + chunk, F32), vmem(chunk, F32), vmem((8,) + chunk, F32),
        vmem((8,) + chunk, F32), vmem((8,) + chunk, F32),
        vmem((3, 64, 256), F32), vmem((4, EDGE, CH), BF16), vmem((4, ROWS, CH), BF16),
        vmem((8,) + small, BF16), vmem((8,) + small, BF16), vmem(small, BF16), vmem((8,) + small, BF16),
        vmem((8,) + small, F32), vmem((8,) + small, F32),
        dma((9,)), dma((1,)), dma((2,)), dma((2,)), dma((9,)), dma((9,)), dma((2,)), dma((2,)), dma((10,)), dma((10,)),
    ] + [dma((8,)) for _ in range(12)]
    early, late = pl.pallas_call(
        kernel,
        out_shape=[jax.ShapeDtypeStruct((3, 64, 256), F32)] * 2,
        in_specs=[anyhow, anyhow, pl.BlockSpec(memory_space=pltpu.SMEM)] + [anyhow] * 7,
        out_specs=[anyhow, pl.BlockSpec(memory_space=pltpu.VMEM)],
        scratch_shapes=scratch,
        compiler_params=pltpu.CompilerParams(
            collective_id=0, has_side_effects=True, vmem_limit_bytes=56 * 1024 * 1024
        ),
    )(
        states[0], noise[0], ws, pw, tw,
        c1.reshape(9 * CH, CH), c2.reshape(9 * CH, CH), aw, pr, ow.T,
    )
    return (early + late)[None]


def solution(mesh):
    image = P("step", None, "quad", None)
    return jax.shard_map(
        body,
        mesh=mesh,
        in_specs=(image, image) + (P(),) * 8,
        out_specs=image,
        check_vma=False,
    )
```

```python
import math

import jax
import jax.numpy as jnp
from jax import lax
from jax.experimental import pallas as pl
from jax.experimental.pallas import tpu as pltpu
from jax.sharding import PartitionSpec as P

CH = 512
HEADS = 8
GROUP = 8
FAR = (5, 4, 3, 7, 2, 6, 1)
PATCH = 8
TEMB = 128
FEAT = 192
GRID = 32
ROWS = 256
EDGE = 32
ALL = ROWS + 2 * EDGE
PLANE = 8
LINES = 8
QUADS = 4
EPS = 1e-05
MESH = pl.DeviceIdType.MESH
F32 = jnp.float32
BF16 = jnp.bfloat16
NT = (((1,), (1,)), ((), ()))


def iota(shape, dim):
    return lax.broadcasted_iota(jnp.int32, shape, dim)


def dot(a, b):
    return jnp.dot(a, b, preferred_element_type=F32)


def dot_nt(a, b):
    return lax.dot_general(a, b, NT, preferred_element_type=F32)


def pack(x):
    low = jnp.concatenate([x[16:24, :128], x[16:24, 128:]], axis=0)
    return jnp.concatenate([x[:16], low], axis=1).astype(BF16)


def unpack(y):
    y = y.astype(F32)
    low = jnp.concatenate([y[:8, 256:], y[8:, 256:]], axis=1)
    return jnp.concatenate([y[:, :256], low], axis=0)


def flat(v):
    return jnp.concatenate([v[i : i + 1] for i in range(4)], axis=1)


def sums_of(x):
    def fold(v):
        v = jnp.sum(v, axis=0, keepdims=True)
        return [v[:, 128 * i : 128 * (i + 1)] for i in range(4)]

    return jnp.concatenate(fold(x) + fold(x * x), axis=0)


def scale_shift(total, count):
    lane = iota((8, 128), 1)
    for s in (1, 2, 4, 8):
        up = pltpu.roll(total, 128 - s, axis=1)
        down = pltpu.roll(total, s, axis=1)
        total = total + jnp.where((lane & s) == 0, up, down)
    total = total / count
    mean, square = total[:4], total[4:]
    rstd = lax.rsqrt(square - mean * mean + EPS)
    shift = -mean * rstd
    return flat(rstd), flat(shift)


def kernel(
    st_h, no_h, ws, pw_h, tw_h, c1_h, c2_h, aw_h, pr_h, ow_h, early, late,
    st, no, pw, tw, c1, c2, aw, pr, ow, wqt, wvt, prt,
    hid, act, inn, blk, blkt, kbuf, vbuf, qz, att, mref, lref, big,
    stat_own, stat_in, e_own, e_in, e_tot, e_line, e_pre, e_out, e_sum, ihalo, raw,
    p_own, p_in, p_tot, p_line, p_pre, p_out,
    load, early_sem, halo_s, halo_r, stat_s, stat_r, inn_s, inn_r, gat_s, gat_r,
    ea_s, ea_r, eb_s, eb_r, ec_s, ec_r, pa_s, pa_r, pb_s, pb_r, pc_s, pc_r,
):
    step = lax.axis_index("step")
    quad = lax.axis_index("quad")
    line = step // PLANE
    spot = step % PLANE


    def at_quad(j):
        return (step, (quad + j) % QUADS)

    def spot_of(j):
        return ((spot // 2 + j // 2) % 4) * 2 + (spot + j) % 2

    def at_spot(j):
        return (line * PLANE + spot_of(j), quad)

    def at_line(j):
        return (((line + j) % LINES) * PLANE + spot, quad)

    barrier = pltpu.get_barrier_semaphore()
    peers = [at_line(j) for j in (4, 3, 5, 2, 6, 1, 7)]
    peers += [at_spot(j) for j in FAR]
    peers += [at_quad(j) for j in range(1, QUADS)]
    for peer in peers:
        pl.semaphore_signal(barrier, inc=1, device_id=peer, device_id_type=MESH)

    def send(src, dst, ss, rs, peer):
        copy = pltpu.make_async_remote_copy(
            src_ref=src, dst_ref=dst, send_sem=ss, recv_sem=rs, device_id=peer, device_id_type=MESH
        )
        copy.start()
        return copy

    loads = [
        pltpu.make_async_copy(st_h, st.at[:, pl.ds(8, 64), :], load.at[0]),
        pltpu.make_async_copy(pw_h, pw, load.at[1]),
        pltpu.make_async_copy(no_h, no, load.at[2]),
        pltpu.make_async_copy(tw_h, tw, load.at[3]),
        pltpu.make_async_copy(c1_h, c1, load.at[4]),
        pltpu.make_async_copy(c2_h, c2, load.at[5]),
        pltpu.make_async_copy(aw_h, aw, load.at[6]),
        pltpu.make_async_copy(pr_h, pr, load.at[7]),
        pltpu.make_async_copy(ow_h, ow, load.at[8]),
    ]
    for item in loads:
        item.start()
    feat = iota((FEAT, ROWS), 0)
    pixel = iota((FEAT, ROWS), 1)
    diag = (feat & 7) == (pixel & 7)
    spread = (iota((FEAT, 24), 0) >> 3 == iota((FEAT, 24), 1)).astype(F32).astype(BF16)
    big[...] = (iota((ROWS, 8 * ROWS), 0) == iota((ROWS, 8 * ROWS), 1) >> 3).astype(F32).astype(BF16)

    def on_diag(v):
        pieces = [v[:, i : i + ROWS] for i in range(0, v.shape[1], ROWS)]
        return jnp.concatenate([jnp.where(diag, piece, 0.0) for piece in pieces], axis=1).astype(BF16)


    loads[0].wait()
    loads[1].wait()

    inside = [st[:, pl.ds(8 * r, 8), :].reshape(24, ROWS) for r in range(1, 9)]
    wide = dot(spread, jnp.concatenate(inside, axis=1).astype(BF16))
    patches = dot_nt(big[...], on_diag(wide)).astype(BF16)
    hid[pl.ds(EDGE, ROWS), :] = dot(patches, pw[...])
    own = pl.ds(EDGE, ROWS)
    stat_own[0] = sums_of(hid[own, :])

    pl.semaphore_wait(barrier, len(peers))
    halo = [
        send(st.at[:, pl.ds(64, 8), :], st.at[:, pl.ds(0, 8), :], halo_s.at[0], halo_r.at[0], at_quad(1)),
        send(st.at[:, pl.ds(8, 8), :], st.at[:, pl.ds(72, 8), :], halo_s.at[1], halo_r.at[1], at_quad(3)),
    ]


    def share_sums(k):
        return [
            send(stat_own.at[k], stat_in.at[k, j - 1], stat_s.at[3 * k + j - 1], stat_r.at[3 * k + j - 1], at_quad(j))
            for j in range(1, QUADS)
        ]

    def total_sums(k, copies):
        total = stat_own[k]
        for j, copy in enumerate(copies):
            copy.wait()
            total = total + stat_in[k, j]
        return scale_shift(total, float(QUADS * ROWS * CH // 32))

    stats = share_sums(0)

    time = 999 - ws[0] - step
    when = jnp.full((8, 128), time.astype(F32))
    place = iota((8, 128), 0) * 128 + iota((8, 128), 1)
    beta_all = 0.0001 + (0.02 - 0.0001) * place.astype(F32) / 999.0
    log_all = jnp.where(place <= time, jnp.log1p(-beta_all), 0.0)
    log_now = jnp.sum(jnp.sum(log_all, axis=1, keepdims=True), axis=0, keepdims=True)
    beta = (0.0001 + (0.02 - 0.0001) * when / 999.0)[:1, :1]
    keep = jnp.exp(log_now)
    root = lax.rsqrt(1.0 - beta)
    of_state = root - 1.0
    of_noise = jnp.sqrt(beta)
    of_pred = -beta * root * lax.rsqrt(1.0 - keep)
    half = TEMB // 2
    lane = iota((8, TEMB), 1)
    angle = when * jnp.exp(-math.log(10000.0) * (lane & (half - 1)).astype(F32) / half)
    embed = jnp.where(lane < half, jnp.cos(angle), jnp.sin(angle)).astype(BF16)
    loads[3].wait()
    embed = dot(embed, tw[...])[:1]
    time_scale, time_shift = 1.0 + embed[:, :CH], embed[:, CH:]

    loads[2].wait()
    head = jnp.where(step == 0, 1.0, 0.0)

    @pl.loop(0, 8)
    def _(r):
        here = st[:, pl.ds(pl.multiple_of(8 * r + 8, 8), 8), :].reshape(24, ROWS)
        push = no[:, pl.ds(pl.multiple_of(8 * r, 8), 8), :].reshape(24, ROWS)
        e_own[r] = (of_state + head) * here + of_noise * push

    def scatter(own_ref, in_ref, ss, rs):
        return [
            send(own_ref.at[spot_of(j)], in_ref.at[spot], ss.at[j], rs.at[j], at_spot(j))
            for j in FAR
        ]

    def to_lines(tot, line_in, ss, rs, start):
        for j in range(1, LINES):
            copy = pltpu.make_async_remote_copy(
                src_ref=tot, dst_ref=line_in.at[j], send_sem=ss.at[j], recv_sem=rs.at[j],
                device_id=at_line(j), device_id_type=MESH,
            )

            @pl.when(line + j < LINES)
            def _():
                if start:
                    copy.start()
                else:
                    copy.wait_send()

            if not start:

                @pl.when(line >= j)
                def _():
                    copy.wait_recv()

    def lines_sum(line_in, shape, load_one):
        base = jnp.zeros(shape, F32)
        for j in range(1, LINES):
            base = base + jnp.where(line >= j, load_one(line_in, j), 0.0)
        return base

    def back(pre, out_ref, ss, rs):
        return [
            send(pre.at[spot_of(j)], out_ref.at[spot], ss.at[j], rs.at[j], at_spot(j))
            for j in FAR
        ]

    early_a = scatter(e_own, e_in, ea_s, ea_r)

    for item in halo:
        item.wait()
    outer = [st[:, pl.ds(8 * r, 8), :].reshape(24, ROWS) for r in (0, 9)]
    wide = on_diag(dot(spread, jnp.concatenate(outer, axis=1).astype(BF16)))
    patches = dot_nt(big[0 : 2 * GRID, 0 : 2 * ROWS], wide).astype(BF16)
    edge_rows = dot(patches, pw[...])
    hid[pl.ds(0, EDGE), :] = edge_rows[:EDGE]
    hid[pl.ds(ALL - EDGE, EDGE), :] = edge_rows[EDGE:]
    scale, shift = total_sums(0, stats)

    def activate(source, gain, bias):
        @pl.loop(0, 10)
        def _(r):
            where = pl.ds(pl.multiple_of(GRID * r, GRID), GRID)
            x = source[where, :] * gain + bias
            outside = ((quad == 0) & (r == 0)) | ((quad == QUADS - 1) & (r == 9))
            x = x * (jnp.tanh(0.5 * x) + 1.0) * jnp.where(outside, 0.0, 0.5)
            col = iota((GRID, CH), 0)
            act[0, where, :] = jnp.where(col == 0, 0.0, pltpu.roll(x, 1, axis=0)).astype(BF16)
            act[1, where, :] = x.astype(BF16)
            act[2, where, :] = jnp.where(col == GRID - 1, 0.0, pltpu.roll(x, GRID - 1, axis=0)).astype(BF16)

    def convolve(weight, n):
        total = None
        for row in range(3):
            for col in range(3):
                term = dot(
                    act[col, pl.ds(GRID * row, ROWS), :],
                    weight[pl.ds((3 * row + col) * CH, CH), pl.ds(256 * n, 256)],
                )
                total = term if total is None else total + term
        return total

    activate(hid, scale, shift)
    loads[4].wait()
    for n in range(2):
        inn[own, pl.ds(256 * n, 256)] = convolve(c1, n)
    stat_own[1] = sums_of(inn[own, :])
    stats = share_sums(1)
    middle = flat(stat_own[1]) / ROWS
    ihalo[0] = (inn[pl.ds(ROWS, EDGE), :] - middle).astype(BF16)
    ihalo[1] = (inn[pl.ds(EDGE, EDGE), :] - middle).astype(BF16)
    edges = [
        send(ihalo.at[0], ihalo.at[2], inn_s.at[0], inn_r.at[0], at_quad(1)),
        send(ihalo.at[1], ihalo.at[3], inn_s.at[1], inn_r.at[1], at_quad(3)),
    ]

    for item in early_a:
        item.wait()
    e_in[spot] = e_own[spot]
    run = jnp.zeros((24, ROWS), F32)
    for d in range(PLANE):
        e_pre[d] = run
        run = run + e_in[d]
    e_tot[...] = run
    to_lines(e_tot, e_line, eb_s, eb_r, True)
    loads[6].wait()
    wqt[...] = aw[:, :CH].T

    scale, shift = total_sums(1, stats)
    for item in edges:
        item.wait()
    inn[pl.ds(0, EDGE), :] = ihalo[2].astype(F32) + flat(stat_in[1, 0]) / ROWS
    inn[pl.ds(ALL - EDGE, EDGE), :] = ihalo[3].astype(F32) + flat(stat_in[1, 2]) / ROWS
    activate(inn, scale * time_scale, shift * time_scale + time_shift)
    loads[5].wait()
    for n in range(2):
        lanes = pl.ds(256 * n, 256)
        blk[:, lanes] = hid[own, lanes] + convolve(c2, n)
    stat_own[2] = sums_of(blk[...])
    stats = share_sums(2)
    raw[0] = (blk[...] - flat(stat_own[2]) / ROWS).astype(BF16)
    low, high = pl.ds(0, 128), pl.ds(128, 128)
    low_r, high_l = [], []
    for i in range(2):
        a, b = pl.ds(64 * i, 64), pl.ds(128 + 64 * i, 64)
        low_r.append(send(raw.at[0, a], raw.at[1, a], gat_s.at[i], gat_r.at[i], at_quad(1)))
        high_l.append(send(raw.at[0, b], raw.at[2, b], gat_s.at[2 + i], gat_r.at[2 + i], at_quad(3)))
    high_r = send(raw.at[0, high], raw.at[1, high], gat_s.at[4], gat_r.at[4], at_quad(1))
    low_l = send(raw.at[0, low], raw.at[2, low], gat_s.at[5], gat_r.at[5], at_quad(3))


    wvt[...] = aw[:, 2 * CH :].T
    loads[7].wait()
    loads[8].wait()
    prt[...] = pr[...].T
    blkt[...] = blk[...].T

    scale, shift = total_sums(2, stats)
    pass_r, pass_l = [], []

    def forward(i):
        a, b = pl.ds(64 * i, 64), pl.ds(128 + 64 * i, 64)
        low_r[i].wait_recv()
        pass_r.append(send(raw.at[1, a], raw.at[3, a], gat_s.at[6 + i], gat_r.at[6 + i], at_quad(1)))
        high_l[i].wait_recv()
        pass_l.append(send(raw.at[2, b], raw.at[3, b], gat_s.at[8 + i], gat_r.at[8 + i], at_quad(3)))

    forward(0)
    normed = (blk[...] * scale + shift).astype(BF16)
    queries = dot_nt(wqt[...], normed).astype(BF16)
    upper = iota((128, ROWS), 0) < 64
    for p in range(4):
        pair = queries[128 * p : 128 * (p + 1)]
        qz[2 * p] = jnp.where(upper, pair, jnp.zeros_like(pair))
        qz[2 * p + 1] = jnp.where(upper, jnp.zeros_like(pair), pair)
    sharp = math.log2(math.e) / 8.0

    def attend(slots, normed=None):
        first, keys = slots == (0,), len(slots) * ROWS
        for i, slot in enumerate(slots):
            if slot > 0:
                offset = flat(stat_in[2, (0, 2, 1)[slot - 1]]) / ROWS * scale + shift
                normed = (raw[slot].astype(F32) * scale + offset).astype(BF16)
            kbuf[pl.ds(ROWS * i, ROWS), :] = dot(normed, aw[:, CH : 2 * CH]).astype(BF16)
            vbuf[:, pl.ds(ROWS * i, ROWS)] = dot_nt(wvt[...], normed).astype(BF16)

        def some(base):
            scores, most, weights, total = {}, {}, {}, {}
            for g in range(GROUP):
                h = base + g
                pair = pl.ds(pl.multiple_of(128 * (h // 2), 128), 128)
                scores[g] = dot(kbuf[0:keys, pair], qz[h])
            for g in range(GROUP):
                h = base + g
                most[g] = jnp.max(scores[g], axis=0, keepdims=True)
                if not first:
                    most[g] = jnp.maximum(most[g], mref[h])
                e = jnp.exp2((scores[g] - most[g]) * sharp)
                total[g] = jnp.sum(e, axis=0, keepdims=True)
                weights[g] = e.astype(BF16)
            for g in range(GROUP):
                h = base + g
                rows = pl.ds(pl.multiple_of(64 * h, 64), 64)
                value = dot(vbuf[rows, 0:keys], weights[g])
                if not first:
                    fade = jnp.exp2((mref[h] - most[g]) * sharp)
                    total[g] = total[g] + lref[h] * fade
                    value = value + att[rows, :] * fade
                mref[h] = most[g]
                lref[h] = total[g]
                att[rows, :] = value

        if GROUP == HEADS:
            some(0)
        else:
            pl.loop(0, HEADS // GROUP)(lambda i: some(i * GROUP))

    forward(1)
    attend((0,), normed)
    to_lines(e_tot, e_line, eb_s, eb_r, False)
    base = lines_sum(e_line, (24, ROWS), lambda ref, j: ref[j])
    for d in range(PLANE):
        e_pre[d] = e_pre[d] + base
    early_c = back(e_pre, e_out, ec_s, ec_r)
    high_r.wait_recv()
    low_l.wait_recv()
    attend((1, 2))
    for item in pass_r + pass_l:
        item.wait_recv()
    attend((3,))
    for h in range(HEADS):
        rows = pl.ds(64 * h, 64)
        att[rows, :] = att[rows, :] / lref[h]

    mixed = blkt[...] + dot(prt[...], att[...].astype(BF16))
    predicted = (dot(ow[...], mixed.astype(BF16)) * of_pred).astype(BF16)
    wide = dot(predicted, big[...])
    wide = lax.dot_general(spread, on_diag(wide), (((0,), (0,)), ((), ())), preferred_element_type=F32)
    for r in range(8):
        p_own[r] = pack(wide[:, 256 * r : 256 * (r + 1)])
    late_a = scatter(p_own, p_in, pa_s, pa_r)
    p_in[spot] = p_own[spot]
    for item in late_a:
        item.wait()
    run = jnp.zeros((16, 384), F32)
    runs = []
    for d in range(PLANE):
        runs.append(run)
        run = run + p_in[d].astype(F32)
    p_tot[...] = run.astype(BF16)
    to_lines(p_tot, p_line, pb_s, pb_r, True)
    for item in early_c:
        item.wait()
    e_out[spot] = e_pre[spot]
    for r in range(8):
        e_sum[:, pl.ds(8 * r, 8), :] = (e_out[r] + e_own[r]).reshape(3, 8, ROWS)
    early_copy = pltpu.make_async_copy(e_sum, early, early_sem.at[0])
    early_copy.start()
    to_lines(p_tot, p_line, pb_s, pb_r, False)
    base = lines_sum(p_line, (16, 384), lambda ref, j: ref[j].astype(F32))
    for d in range(PLANE):
        p_pre[d] = runs[d] + base
    late_c = back(p_pre, p_out, pc_s, pc_r)
    p_out[spot] = p_pre[spot]
    for item in late_c:
        item.wait()
    for r in range(8):
        late[:, pl.ds(8 * r, 8), :] = (unpack(p_out[r]) + unpack(p_own[r])).reshape(3, 8, ROWS)
    early_copy.wait()
    for item in low_r + high_l + [high_r, low_l] + pass_r + pass_l:
        item.wait_send()


def body(states, noise, ws, pw, tw, c1, c2, aw, pr, ow):
    dma = pltpu.SemaphoreType.DMA
    vmem = pltpu.VMEM
    anyhow = pl.BlockSpec(memory_space=pl.ANY)
    chunk, small = (24, ROWS), (16, 384)
    scratch = [
        vmem((3, 80, 256), F32), vmem((3, 64, 256), F32),
        vmem((FEAT, CH), BF16), vmem((TEMB, 2 * CH), BF16),
        vmem((9 * CH, CH), BF16), vmem((9 * CH, CH), BF16),
        vmem((CH, 3 * CH), BF16), vmem((CH, CH), BF16), vmem((FEAT, CH), BF16),
        vmem((CH, CH), BF16), vmem((CH, CH), BF16), vmem((CH, CH), BF16),
        vmem((ALL, CH), F32), vmem((3, ALL, CH), BF16), vmem((ALL, CH), F32),
        vmem((ROWS, CH), F32), vmem((CH, ROWS), F32),
        vmem((2 * ROWS, CH), BF16), vmem((CH, 2 * ROWS), BF16),
        vmem((8, 128, ROWS), BF16), vmem((CH, ROWS), F32),
        vmem((8, 1, ROWS), F32), vmem((8, 1, ROWS), F32), vmem((ROWS, 8 * ROWS), BF16),
        vmem((3, 8, 128), F32), vmem((3, 3, 8, 128), F32),
        vmem((8,) + chunk, F32), vmem((8,) + chunk, F32), vmem(chunk, F32), vmem((8,) + chunk, F32),
        vmem((8,) + chunk, F32), vmem((8,) + chunk, F32),
        vmem((3, 64, 256), F32), vmem((4, EDGE, CH), BF16), vmem((4, ROWS, CH), BF16),
        vmem((8,) + small, BF16), vmem((8,) + small, BF16), vmem(small, BF16), vmem((8,) + small, BF16),
        vmem((8,) + small, F32), vmem((8,) + small, F32),
        dma((9,)), dma((1,)), dma((2,)), dma((2,)), dma((9,)), dma((9,)), dma((2,)), dma((2,)), dma((10,)), dma((10,)),
    ] + [dma((8,)) for _ in range(12)]
    early, late = pl.pallas_call(
        kernel,
        out_shape=[jax.ShapeDtypeStruct((3, 64, 256), F32)] * 2,
        in_specs=[anyhow, anyhow, pl.BlockSpec(memory_space=pltpu.SMEM)] + [anyhow] * 7,
        out_specs=[anyhow, pl.BlockSpec(memory_space=pltpu.VMEM)],
        scratch_shapes=scratch,
        compiler_params=pltpu.CompilerParams(
            collective_id=0, has_side_effects=True, vmem_limit_bytes=56 * 1024 * 1024
        ),
    )(
        states[0], noise[0], ws, pw, tw,
        c1.reshape(9 * CH, CH), c2.reshape(9 * CH, CH), aw, pr, ow.T,
    )
    return (early + late)[None]


def solution(mesh):
    image = P("step", None, "quad", None)
    return jax.shard_map(
        body,
        mesh=mesh,
        in_specs=(image, image) + (P(),) * 8,
        out_specs=image,
        check_vma=False,
    )
```
